32 devices in a mesh: row: 4 (over y, core), col: 8 (over z, x).
Axes of the slice: x: 2, y: 2, z: 4, core: 2. Of those that a mesh axis runs over, the one named last changes fastest.
Arguments:
- stream_speed: bfloat16 [512, 2048, 32], P('col', 'row'), may hold values from -6 to 6
- normal_speed: bfloat16 [512, 2048, 32], P('col', 'row'), may hold values from -6 to 6
- span_speed: bfloat16 [512, 2048, 32], P('col', 'row'), may hold values from -6 to 6
- stream_first: bfloat16 [2048, 2048], P('row'), may hold values from -0.125 to 0.125
- stream_second: bfloat16 [2048, 2048], P('row'), may hold values from -0.125 to 0.125
- wall_first: bfloat16 [512, 512], replicated, may hold values from -0.25 to 0.25
- wall_second: bfloat16 [512, 512], replicated, may hold values from -0.25 to 0.25
- metric1: float32 [512], replicated, may hold values from 0.5 to 2
- metric2: float32 [512], replicated, may hold values from -1.5 to 1.5
- span_coef: float32 [2, 9], replicated, may hold values from -1 to 1
- counts: int32 [8], replicated, may hold values from 1 to 4, as said below
Outputs:
- tendency: bfloat16 [512, 2048, 32], P('col', 'row')
The draws below stay inside these ranges and needn't reach their ends.
Inputs may be any that keep to these rules, and one draw needn't show every extreme that they name: counts[b] is the number of fluid planes at the start of spanwise block b of 4 planes; some block is all fluid.
All inputs are finite; a program needn't handle non-finite values.
Results may differ from the reference program's by a relative error of at most 0.0051.
Values may be sent and summed in bfloat16 or wider, within the bound.
No kernel may reach another device: no remote copies, remote signals or barrier semaphores. Data moves between devices by JAX's collectives and lax.ppermute only.
A program may use at most 192 MiB of HBM per device.

```python
import math
import jax
import jax.numpy as jnp
from jax import lax

NX = 2048
NY = 512
ZB = 4
REACH = 4
NZ = 32


def draw_counts(key, part):
    block_total = NZ // ZB
    first_key, second_key = jax.random.split(jax.random.fold_in(key, 17))
    values = jax.random.randint(first_key, (block_total,), 1, ZB + 1)
    chosen = jax.random.randint(second_key, (), 0, block_total)
    return jnp.where(jnp.arange(block_total) == chosen, ZB, values).astype(jnp.int32)


def levels(rng, shape, shards, smallest, high):
    level, own = 1.0, jax.random.fold_in(rng, 6)
    for position, parts in shards:
        draws = jnp.exp(jax.random.uniform(jax.random.fold_in(own, position), (parts,), jnp.float32, smallest / len(shards), high / len(shards)))
        level = level * jnp.repeat(draws, shape[position] // parts).reshape([-1 if axis == position else 1 for axis in range(len(shape))])
    return level


def scatter_about(own_key, shape, width, most, shards=(), kind=jnp.bfloat16):
    values = jax.random.normal(own_key, shape, jnp.float32) * width
    if len(shards) > 0:
        values = levels(own_key, shape, shards, -0.22, 0.18) * values
    return jnp.clip(values, min=-most, max=most).astype(kind)


def setup_inputs(seed: int = 0) -> dict:
    streams_of = jax.random.split(jax.random.key(seed), 12)
    stream_speed = scatter_about(streams_of[0], (NY, NX, NZ), 1.0, 6.0, ((0, 8), (1, 4)))
    normal_speed = scatter_about(streams_of[1], (NY, NX, NZ), 1.0, 6.0, ((0, 8), (1, 4)))
    span_speed = scatter_about(streams_of[2], (NY, NX, NZ), 1.0, 6.0, ((0, 8), (1, 4)))
    stream_first = scatter_about(streams_of[3], (NX, NX), NX ** -0.5, 0.125, ((0, 4),))
    stream_second = scatter_about(streams_of[4], (NX, NX), NX ** -0.5, 0.125, ((0, 4),))
    wall_first = scatter_about(streams_of[5], (NY, NY), NY ** -0.5, 0.25)
    wall_second = scatter_about(streams_of[6], (NY, NY), NY ** -0.5, 0.25)
    metric1 = jnp.clip(jnp.exp(jax.random.uniform(streams_of[7], (NY,), jnp.float32, math.log(0.5), math.log(2.0))), 0.5, 2.0)
    metric2 = jnp.clip(jax.random.uniform(streams_of[8], (NY,), jnp.float32, -1.5, 1.5), -1.5, 1.5)
    span_coef = jnp.clip(jax.random.uniform(streams_of[9], (2, 2 * REACH + 1), jnp.float32, -1.0, 1.0), -1.0, 1.0)
    counts = draw_counts(jax.random.fold_in(streams_of[11], 71), 0)
    return dict(stream_speed=stream_speed, normal_speed=normal_speed, span_speed=span_speed, stream_first=stream_first, stream_second=stream_second, wall_first=wall_first, wall_second=wall_second, metric1=metric1, metric2=metric2, span_coef=span_coef, counts=counts)


viscosity = 0.25


def along_stream(matrix, field):
    flattened = jnp.transpose(field, (1, 0, 2)).reshape(NX, -1)
    outcome = jnp.dot(matrix, flattened, preferred_element_type=jnp.float32)
    return jnp.transpose(outcome.reshape(NX, NY, NZ), (1, 0, 2))


def reference(stream_speed, normal_speed, span_speed, stream_first, stream_second, wall_first, wall_second, metric1, metric2, span_coef, counts):
    stream_full = stream_speed.astype(jnp.float32)
    flux_stream = (stream_full * stream_full).astype(jnp.bfloat16)
    term_stream = viscosity * along_stream(stream_second, stream_speed) - along_stream(stream_first, flux_stream)
    flux_normal = (stream_full * normal_speed.astype(jnp.float32)).astype(jnp.bfloat16)
    flattened = stream_speed.reshape(NY, -1)
    first_stream = jnp.dot(wall_first, flattened, preferred_element_type=jnp.float32)
    second_stream = jnp.dot(wall_second, flattened, preferred_element_type=jnp.float32)
    first_flux = jnp.dot(wall_first, flux_normal.reshape(NY, -1), preferred_element_type=jnp.float32)
    weight_one = metric1[:, None]
    weight_two = metric2[:, None]
    term_wall = viscosity * (weight_one * weight_one * second_stream + weight_two * first_stream) - weight_one * first_flux
    term_wall = lax.optimization_barrier(term_wall.reshape(NY, NX, NZ).astype(jnp.bfloat16)).astype(jnp.float32)
    flux_span = lax.optimization_barrier((stream_full * span_speed.astype(jnp.float32)).astype(jnp.bfloat16)).astype(jnp.float32)
    radius = span_coef.shape[1] // 2
    term_span = jnp.zeros((NY, NX, NZ), jnp.float32)
    for offset_z in range(-radius, radius + 1):
        term_span = term_span + viscosity * span_coef[1, offset_z + radius] * jnp.roll(stream_full, -offset_z, 2)
        term_span = term_span - span_coef[0, offset_z + radius] * jnp.roll(flux_span, -offset_z, 2)
    plane_index = jnp.arange(NZ, dtype=jnp.int32)
    fluid_limit = counts[(plane_index // ZB).astype(jnp.int32)]
    fluid_mask = (plane_index % ZB < fluid_limit).astype(jnp.float32)
    return (fluid_mask * (term_stream + term_wall + term_span)).astype(jnp.bfloat16)
```

```python
import functools
import math

import jax
import jax.numpy as jnp
from jax import lax
from jax.experimental import pallas as pl
from jax.experimental.pallas import tpu as pltpu
from jax.sharding import PartitionSpec as P

ZB = 4
LANES = 128
ROWS = 16
HALF = 8
CHUNK = 32
VISCOSITY = 0.25
VMEM_BYTES = 63 * 1024 * 1024


def params(steps):
    return pltpu.CompilerParams(
        dimension_semantics=("arbitrary",) * steps, vmem_limit_bytes=VMEM_BYTES
    )


def unit_lanes(width):
    return LANES if width % LANES == 0 else width


def step_rows(rows):
    return next(g for g in (2 * ROWS, ROWS, rows) if rows % g == 0)


def list_fluid(counts_ref, order_ref):
    planes = order_ref.shape[0]

    def clear(plane, carry):
        order_ref[plane] = 0
        return carry

    lax.fori_loop(0, planes, clear, 0)

    def visit(plane, filled):
        fluid = lax.rem(plane, ZB) < counts_ref[plane // ZB]

        @pl.when(fluid)
        def _():
            order_ref[filled] = plane

        return filled + fluid.astype(jnp.int32)

    return lax.fori_loop(0, planes, visit, 0)


def one_hot_rows(matrix_ref, order, rows, planes, found):
    spread = (2 * rows, rows * planes)
    row = lax.broadcasted_iota(jnp.int32, spread, 0)
    later = row >= rows
    near = lax.broadcasted_iota(jnp.int32, spread, 1) - planes * jnp.where(later, row - rows, row)

    def one(pair, carry):
        slot = 2 * pair
        here = jnp.where(slot < found, order[slot], -rows * planes)
        after = jnp.where(slot + 1 < found, order[slot + 1], -rows * planes)
        hot = jnp.where(near == jnp.where(later, after, here), 1.0, 0.0).astype(jnp.bfloat16)
        start = pl.multiple_of(slot * rows, 2 * rows)
        matrix_ref[pl.ds(start, 2 * rows), :] = hot
        return carry

    lax.fori_loop(0, matrix_ref.shape[0] // (2 * rows), one, 0)


def pack_kernel(counts_ref, spot_ref, u_ref, v_ref, own_ref, *refs):
    *pair_refs, order, chosen = refs
    rows, planes, width = u_ref.shape
    kept = own_ref.shape[0]
    parts, apart, _, _, lanes = pair_refs[0].shape

    @pl.when(pl.program_id(0) == 0)
    def _():
        found = list_fluid(counts_ref, order)
        one_hot_rows(chosen, order, HALF, planes, found)

    def select(ref, first):
        picked = []
        for start in range(0, ROWS, HALF):
            flat = ref[pl.ds(first + start, HALF)].reshape(HALF * planes, width)
            part = jnp.dot(chosen[...], flat, preferred_element_type=jnp.float32)
            picked.append(part.reshape(kept, HALF, width))
        return jnp.concatenate(picked, axis=1).astype(jnp.bfloat16)

    def some(index, carry):
        first = pl.multiple_of(index * ROWS, ROWS)
        here = pl.ds(first, ROWS)
        for field, ref in enumerate((u_ref, v_ref)):
            value = select(ref, first)
            if field == 0:
                own_ref[:, here] = value
            for part in range(parts):
                lane = slice(part * lanes, (part + 1) * lanes)
                pair_refs[0][part, :, field, here] = value[:apart, :, lane]
                if len(pair_refs) > 1:
                    pair_refs[1][part ^ spot_ref[0], :, field, here] = value[apart:, :, lane]
        return carry

    lax.fori_loop(0, rows // ROWS, some, 0)


def pack(counts, spot, u, v, apart, kept):
    rows, planes, width = u.shape
    lanes = unit_lanes(width)
    parts = width // lanes
    group = step_rows(rows)
    sizes = [size for size in (apart, kept - apart) if size > 0]
    return pl.pallas_call(
        pack_kernel,
        grid=(rows // group,),
        out_shape=[jax.ShapeDtypeStruct((kept, rows, width), jnp.bfloat16)]
        + [jax.ShapeDtypeStruct((parts, size, 2, rows, lanes), jnp.bfloat16) for size in sizes],
        in_specs=[
            pl.BlockSpec(memory_space=pltpu.SMEM),
            pl.BlockSpec(memory_space=pltpu.SMEM),
            pl.BlockSpec((group, planes, width), lambda i: (i, 0, 0)),
            pl.BlockSpec((group, planes, width), lambda i: (i, 0, 0)),
        ],
        out_specs=[pl.BlockSpec((kept, group, width), lambda i: (0, i, 0))]
        + [
            pl.BlockSpec((parts, size, 2, group, lanes), lambda i: (0, 0, 0, i, 0))
            for size in sizes
        ],
        scratch_shapes=[
            pltpu.SMEM((planes,), jnp.int32),
            pltpu.VMEM((kept * HALF, HALF * planes), jnp.bfloat16),
        ],
        compiler_params=params(1),
        name="pack",
    )(counts, spot, u, v)


def band_rows(matrix_ref, coef_ref, order, rows, planes):
    taps = coef_ref.shape[1]
    span = rows * planes
    spread = (2 * rows, span)
    row = lax.broadcasted_iota(jnp.int32, spread, 0)
    later = row >= rows
    plane = lax.broadcasted_iota(jnp.int32, spread, 1) - planes * jnp.where(later, row - rows, row)
    inside = (plane >= 0) & (plane < planes)

    def one(pair, carry):
        slot = 2 * pair
        ahead = plane - jnp.where(later, order[slot + 1], order[slot]) + taps // 2
        ahead = jnp.where(ahead < 0, ahead + planes, ahead)
        ahead = jnp.where(ahead >= planes, ahead - planes, ahead)
        ahead = jnp.where(inside, ahead, -1)
        start = pl.multiple_of(slot * rows, 2 * rows)

        def tap(index, values):
            hit = ahead == index
            on_u, on_f = VISCOSITY * coef_ref[1, index], -coef_ref[0, index]
            return (
                values[0] + jnp.where(hit, on_u, 0.0),
                values[1] + jnp.where(hit, on_f, 0.0),
            )

        zero = jnp.zeros(spread, jnp.float32)
        for field, value in enumerate(lax.fori_loop(0, taps, tap, (zero, zero), unroll=True)):
            high = value.astype(jnp.bfloat16)
            low = (value - high.astype(jnp.float32)).astype(jnp.bfloat16)
            matrix_ref[0, pl.ds(start, 2 * rows), field * span : (field + 1) * span] = high
            matrix_ref[1, pl.ds(start, 2 * rows), field * span : (field + 1) * span] = low
        return carry

    lax.fori_loop(0, matrix_ref.shape[1] // (2 * rows), one, 0)


def span_kernel(counts_ref, coef_ref, u_ref, w_ref, out_ref, order, bands):
    rows, planes, width = u_ref.shape
    kept = out_ref.shape[0]

    @pl.when(pl.program_id(0) == 0)
    def _():
        list_fluid(counts_ref, order)
        band_rows(bands, coef_ref, order, HALF, planes)

    def some(index, carry):
        here = pl.ds(pl.multiple_of(index * HALF, HALF), HALF)
        u = u_ref[here].reshape(HALF * planes, width)
        w = w_ref[here].reshape(HALF * planes, width)
        flux = (u.astype(jnp.float32) * w.astype(jnp.float32)).astype(jnp.bfloat16)
        fields = jnp.concatenate([u, flux], axis=0)
        acc = jnp.dot(bands[0], fields, preferred_element_type=jnp.float32)
        acc = acc + jnp.dot(bands[1], fields, preferred_element_type=jnp.float32)
        out_ref[:, here] = acc.reshape(kept, HALF, width)
        return carry

    lax.fori_loop(0, rows // HALF, some, 0)


def span_terms(counts, coef, u, w, kept):
    rows, planes, width = u.shape
    group = step_rows(rows)
    return pl.pallas_call(
        span_kernel,
        grid=(rows // group,),
        out_shape=jax.ShapeDtypeStruct((kept, rows, width), jnp.float32),
        in_specs=[
            pl.BlockSpec(memory_space=pltpu.SMEM),
            pl.BlockSpec(memory_space=pltpu.SMEM),
            pl.BlockSpec((group, planes, width), lambda i: (i, 0, 0)),
            pl.BlockSpec((group, planes, width), lambda i: (i, 0, 0)),
        ],
        out_specs=pl.BlockSpec((kept, group, width), lambda i: (0, i, 0)),
        scratch_shapes=[
            pltpu.SMEM((planes,), jnp.int32),
            pltpu.VMEM((2, kept * HALF, 2 * HALF * planes), jnp.bfloat16),
        ],
        compiler_params=params(1),
        cost_estimate=pl.CostEstimate(
            flops=8 * kept * HALF * planes * rows * width,
            bytes_accessed=8 * kept * rows * width,
            transcendentals=0,
        ),
        name="span_terms",
    )(counts, coef, u, w)


def stream_kernel(spots_ref, *refs):
    *block_refs, first_ref, second_ref, span_ref, out_ref, matrix, both = refs
    group, rows, width = block_refs[0].shape
    own = first_ref.shape[0]
    places = len(block_refs)

    @pl.when(pl.program_id(0) == 0)
    def _():
        def prepare(place, carry):
            lane = pl.ds(pl.multiple_of(spots_ref[place] * width, width), width)

            def some(index, carry):
                row = pl.ds(pl.multiple_of(index * CHUNK, CHUNK), CHUNK)
                matrix[place, row, :width] = second_ref[row, lane] * jnp.bfloat16(VISCOSITY)
                matrix[place, row, width:] = -first_ref[row, lane]
                return carry

            return lax.fori_loop(0, own // CHUNK, some, carry)

        lax.fori_loop(0, places, prepare, 0)

    for place, ref in enumerate(block_refs):

        def square(slot, carry):
            u = ref[slot]
            full = u.astype(jnp.float32)
            row = pl.ds(pl.multiple_of(slot * rows, rows), rows)
            both[place, row, :width] = u
            both[place, row, width:] = (full * full).astype(jnp.bfloat16)
            return carry

        lax.fori_loop(0, group, square, 0)

    out_ref[...] = span_ref[...]

    def one(place, carry):
        part = lax.dot_general(
            both[place],
            matrix[place],
            (((1,), (1,)), ((), ())),
            preferred_element_type=jnp.float32,
        )
        out_ref[...] += part.reshape(out_ref.shape)
        return carry

    lax.fori_loop(0, places, one, 0)


def stream_terms(spots, blocks, first, second, span):
    kept, rows, width = blocks[0].shape
    own, total = first.shape
    group = min(4, kept)
    by_group = pl.BlockSpec((group, rows, width), lambda i: (i, 0, 0))
    whole = pl.BlockSpec((own, total), lambda i: (0, 0))
    return pl.pallas_call(
        stream_kernel,
        grid=(pl.cdiv(kept, group),),
        out_shape=jax.ShapeDtypeStruct((kept, rows, own), jnp.float32),
        in_specs=[pl.BlockSpec(memory_space=pltpu.SMEM)]
        + [by_group] * len(blocks)
        + [whole, whole, pl.BlockSpec((group, rows, own), lambda i: (i, 0, 0))],
        out_specs=pl.BlockSpec((group, rows, own), lambda i: (i, 0, 0)),
        scratch_shapes=[
            pltpu.VMEM((len(blocks), own, 2 * width), jnp.bfloat16),
            pltpu.VMEM((len(blocks), group * rows, 2 * width), jnp.bfloat16),
        ],
        compiler_params=params(1),
        cost_estimate=pl.CostEstimate(
            flops=4 * kept * rows * own * total,
            bytes_accessed=2 * kept * rows * total + 4 * own * total,
            transcendentals=0,
        ),
        name="stream_terms",
    )(spots, *blocks, first, second, span)


def gather_rows(own, span):
    count = lax.axis_size("row")
    blocks, spots = [own], [lax.axis_index("row")]
    bit = count // 2
    while bit > 0:
        pairs = [(row, row ^ bit) for row in range(count)]
        blocks = blocks + [lax.ppermute(block, "row", pairs) for block in blocks]
        spots = spots + [spot ^ bit for spot in spots]
        blocks[-1], span = lax.optimization_barrier((blocks[-1], span))
        bit //= 2
    return blocks, jnp.stack(spots).astype(jnp.int32), span


def wall_kernel(whole_steps, spot_ref, matrix_ref, pair_ref, *refs):
    *half_refs, out_ref, lines = refs
    sources, group, _, rows, lanes = pair_ref.shape
    total = sources * rows
    step = pl.program_id(0)
    pack_units = 2 if group % 2 == 0 else 1

    def both(u, v):
        return u, (u.astype(jnp.float32) * v.astype(jnp.float32)).astype(jnp.bfloat16)

    def put(unit, terms):
        terms = terms.astype(jnp.bfloat16)
        for k in range(pack_units):
            lane = slice(k * lanes, (k + 1) * lanes)
            out_ref[:, unit + k] = terms[:, lane].reshape(sources, rows, lanes)

    @pl.when(step < whole_steps)
    def _():
        def some(index, carry):
            unit = index * pack_units
            for k in range(pack_units):
                u, flux = both(pair_ref[:, unit + k, 0], pair_ref[:, unit + k, 1])
                lane = slice(k * lanes, (k + 1) * lanes)
                lines[:total, lane] = u.reshape(total, lanes)
                lines[total:, lane] = flux.reshape(total, lanes)
            put(unit, jnp.dot(matrix_ref[...], lines[...], preferred_element_type=jnp.float32))
            return carry

        lax.fori_loop(0, group // pack_units, some, 0)

    if len(half_refs) == 0:
        return
    near = total // 2

    @pl.when(step >= whole_steps)
    def _():
        def some(index, carry):
            unit = index * pack_units
            for mask, ref in enumerate(half_refs):
                start = pl.multiple_of((spot_ref[0] ^ mask) * rows, rows)
                for k in range(pack_units):
                    u, flux = both(ref[unit + k, 0], ref[unit + k, 1])
                    lane = slice(k * lanes, (k + 1) * lanes)
                    lines[pl.ds(start, rows), lane] = u
                    lines[pl.ds(start + near, rows), lane] = flux
            on_u = pl.ds(pl.multiple_of(spot_ref[1] * near, near), near)
            on_flux = pl.ds(pl.multiple_of(total + spot_ref[1] * near, near), near)
            terms = jnp.dot(
                matrix_ref[:, on_u], lines[:near], preferred_element_type=jnp.float32
            ) + jnp.dot(
                matrix_ref[:, on_flux], lines[near : 2 * near], preferred_element_type=jnp.float32
            )
            put(unit, terms)
            return carry

        lax.fori_loop(0, group // pack_units, some, 0)


def wall_terms(spot, matrix, pairs, halves):
    sources, units, _, rows, lanes = pairs.shape
    more = halves[0].shape[0] if halves else 0
    group = next(g for g in (4, 6, 10, 2, 1) if units % g == 0)
    whole_steps = units // group
    pack_units = 2 if group % 2 == 0 else 1
    half_blocks = [
        pl.BlockSpec((group, 2, rows, lanes), lambda i: (jnp.maximum(i - whole_steps, 0), 0, 0, 0))
    ] * len(halves)
    return pl.pallas_call(
        functools.partial(wall_kernel, whole_steps),
        grid=(whole_steps + pl.cdiv(more, group),),
        out_shape=jax.ShapeDtypeStruct((sources, units + more, rows, lanes), jnp.bfloat16),
        in_specs=[
            pl.BlockSpec(memory_space=pltpu.SMEM),
            pl.BlockSpec(matrix.shape, lambda i: (0, 0)),
            pl.BlockSpec(
                (sources, group, 2, rows, lanes),
                lambda i: (0, jnp.minimum(i, whole_steps - 1), 0, 0, 0),
            ),
        ]
        + half_blocks,
        out_specs=pl.BlockSpec((sources, group, rows, lanes), lambda i: (0, i, 0, 0)),
        scratch_shapes=[pltpu.VMEM((2 * sources * rows, pack_units * lanes), jnp.bfloat16)],
        compiler_params=params(1),
        cost_estimate=pl.CostEstimate(
            flops=2 * matrix.size * units * lanes,
            bytes_accessed=6 * sources * units * rows * lanes,
            transcendentals=0,
        ),
        name="wall_terms",
    )(spot, matrix, pairs, *halves)


def finish_kernel(apart, counts_ref, base_ref, wall_ref, out_ref, order, chosen, placed):
    rows, planes, width = out_ref.shape
    kept = base_ref.shape[0]
    places, units, _, lanes = wall_ref.shape
    parts = width // lanes
    whole = parts * apart // places

    @pl.when(pl.program_id(0) == 0)
    def _():
        found = list_fluid(counts_ref, order)
        one_hot_rows(chosen, order, HALF, planes, found)
        placed[...] = chosen[...].T

    def some(index, carry):
        here = pl.ds(pl.multiple_of(index * ROWS, ROWS), ROWS)
        columns = []
        for part in range(parts):
            first = part * places // parts
            pieces = [wall_ref[first + k, :whole, here] for k in range(places // parts)]
            column = jnp.concatenate(pieces, axis=0).astype(jnp.float32)
            if units > whole:
                low = wall_ref[part, whole:, here].astype(jnp.float32)
                high = wall_ref[part + parts, whole:, here].astype(jnp.float32)
                column = jnp.concatenate([column, low + high], axis=0)
            columns.append(column)
        value = base_ref[:, here] + jnp.concatenate(columns, axis=-1)
        for start in range(0, ROWS, HALF):
            some_rows = value[:, start : start + HALF].reshape(kept * HALF, width)
            out = jnp.dot(
                placed[...], some_rows.astype(jnp.bfloat16), preferred_element_type=jnp.float32
            )
            out_ref[pl.ds(index * ROWS + start, HALF)] = out.astype(jnp.bfloat16).reshape(
                HALF, planes, width
            )
        return carry

    lax.fori_loop(0, rows // ROWS, some, 0)


def finish(counts, base, wall, planes, apart):
    kept, rows, width = base.shape
    places, units, _, lanes = wall.shape
    group = step_rows(rows)
    return pl.pallas_call(
        functools.partial(finish_kernel, apart),
        grid=(rows // group,),
        out_shape=jax.ShapeDtypeStruct((rows, planes, width), jnp.bfloat16),
        in_specs=[
            pl.BlockSpec(memory_space=pltpu.SMEM),
            pl.BlockSpec((kept, group, width), lambda i: (0, i, 0)),
            pl.BlockSpec((places, units, group, lanes), lambda i: (0, 0, i, 0)),
        ],
        out_specs=pl.BlockSpec((group, planes, width), lambda i: (i, 0, 0)),
        scratch_shapes=[
            pltpu.SMEM((planes,), jnp.int32),
            pltpu.VMEM((kept * HALF, HALF * planes), jnp.bfloat16),
            pltpu.VMEM((HALF * planes, kept * HALF), jnp.bfloat16),
        ],
        compiler_params=params(1),
        name="finish",
    )(counts, base, wall)


def with_kept(
    apart, kept, u, v, w, first, second, wall_first, wall_second, metric1, metric2, coef, counts
):
    rows, planes, width = u.shape
    columns = lax.axis_size("col")
    column = lax.axis_index("col")
    near = columns // 2
    spot = jnp.stack([column % near, column // near]).astype(jnp.int32)
    own, *pairs = pack(counts, spot, u, v, apart, kept)
    parts, lanes = pairs[0].shape[0], pairs[0].shape[-1]
    units = parts * apart // columns
    lines = lax.all_to_all(
        pairs[0].reshape(columns, units, 2, rows, lanes), "col", split_axis=0, concat_axis=0
    )
    halves = [
        pair if mask == 0 else lax.ppermute(pair, "col", [(c, c ^ mask) for c in range(columns)])
        for rest in pairs[1:]
        for mask, pair in enumerate(rest)
    ]
    span = span_terms(counts, coef, u, w, kept)
    blocks, spots, span = gather_rows(own, span)
    one, two = metric1[:, None], metric2[:, None]
    wide_first = wall_first.astype(jnp.float32)
    on_stream = VISCOSITY * (one * one * wall_second.astype(jnp.float32) + two * wide_first)
    matrix = jnp.concatenate([on_stream, -one * wide_first], axis=1).astype(jnp.bfloat16)
    lines, blocks, span = lax.optimization_barrier((lines, blocks, span))
    wall = wall_terms(spot, matrix, lines, halves)
    wall = lax.all_to_all(wall, "col", split_axis=0, concat_axis=0)
    base = stream_terms(spots, blocks, first, second, span)
    return finish(counts, base, wall, planes, apart)


def share_of(kept, parts, columns):
    if 2 * parts != columns:
        return kept
    options = range(columns // 2, kept + 1, columns // 2)
    return min(options, key=lambda a: max(2 * a, 1.5 * a + kept - a) + a + 2 * (kept - a))


def on_device(u, v, w, first, second, wall_first, wall_second, metric1, metric2, coef, counts):
    u, v, w = (jnp.swapaxes(t, 1, 2) for t in (u, v, w))
    planes, width = u.shape[1:]
    columns = lax.axis_size("col")
    parts = width // unit_lanes(width)
    step = 2 if 2 * parts == columns else columns // math.gcd(columns, parts)
    least = counts.shape[0] - 1 + ZB
    low = -(-least // step)
    high = -(-planes // step)
    sizes = [min(size * step, planes) for size in range(low, high + 1)]
    branches = [
        functools.partial(with_kept, share_of(size, parts, columns), size) for size in sizes
    ]
    size = (jnp.sum(counts) + (step - 1)) // step
    operands = (u, v, w, first, second, wall_first, wall_second, metric1, metric2, coef, counts)
    out = lax.switch(size - low, branches, *operands)
    return jnp.swapaxes(out, 1, 2)


def solution(mesh):
    field = P("col", "row", None)
    placed = (field, field, field, P("row", None), P("row", None)) + (P(),) * 6
    return jax.shard_map(
        on_device,
        mesh=mesh,
        in_specs=placed,
        out_specs=field,
        check_vma=False,
    )
```

```python
import functools
import math

import jax
import jax.numpy as jnp
from jax import lax
from jax.experimental import pallas as pl
from jax.experimental.pallas import tpu as pltpu
from jax.sharding import PartitionSpec as P

ZB = 4
LANES = 128
ROWS = 16
HALF = 8
CHUNK = 32
VISCOSITY = 0.25
VMEM_BYTES = 63 * 1024 * 1024
NO_COST = pl.CostEstimate(flops=0, bytes_accessed=0, transcendentals=0)


def params(steps):
    return pltpu.CompilerParams(
        dimension_semantics=("arbitrary",) * steps, vmem_limit_bytes=VMEM_BYTES
    )


def unit_lanes(width):
    return LANES if width % LANES == 0 else width


def step_rows(rows):
    return next(g for g in (2 * ROWS, ROWS, rows) if rows % g == 0)


def list_fluid(counts_ref, order_ref):
    planes = order_ref.shape[0]

    def clear(plane, carry):
        order_ref[plane] = 0
        return carry

    lax.fori_loop(0, planes, clear, 0)

    def visit(plane, filled):
        fluid = lax.rem(plane, ZB) < counts_ref[plane // ZB]

        @pl.when(fluid)
        def _():
            order_ref[filled] = plane

        return filled + fluid.astype(jnp.int32)

    return lax.fori_loop(0, planes, visit, 0)


def one_hot_rows(matrix_ref, order, rows, planes, found):
    spread = (2 * rows, rows * planes)
    row = lax.broadcasted_iota(jnp.int32, spread, 0)
    later = row >= rows
    near = lax.broadcasted_iota(jnp.int32, spread, 1) - planes * jnp.where(later, row - rows, row)

    def one(pair, carry):
        slot = 2 * pair
        here = jnp.where(slot < found, order[slot], -rows * planes)
        after = jnp.where(slot + 1 < found, order[slot + 1], -rows * planes)
        hot = jnp.where(near == jnp.where(later, after, here), 1.0, 0.0).astype(jnp.bfloat16)
        start = pl.multiple_of(slot * rows, 2 * rows)
        matrix_ref[pl.ds(start, 2 * rows), :] = hot
        return carry

    lax.fori_loop(0, matrix_ref.shape[0] // (2 * rows), one, 0)


def pack_kernel(counts_ref, spot_ref, u_ref, v_ref, own_ref, pair_ref, *refs):
    *half_refs, order, chosen, rest = refs
    rows, planes, width = u_ref.shape
    kept = own_ref.shape[0]
    parts, apart, _, _, lanes = pair_ref.shape

    @pl.when(pl.program_id(0) == 0)
    def _():
        found = list_fluid(counts_ref, order)
        one_hot_rows(chosen, order, HALF, planes, found)

    def select(ref, first):
        picked = []
        for start in range(0, ROWS, HALF):
            flat = ref[pl.ds(first + start, HALF)].reshape(HALF * planes, width)
            part = jnp.dot(chosen[...], flat, preferred_element_type=jnp.float32)
            picked.append(part.reshape(kept, HALF, width))
        return jnp.concatenate(picked, axis=1).astype(jnp.bfloat16)

    def some(index, carry):
        first = pl.multiple_of(index * ROWS, ROWS)
        here = pl.ds(first, ROWS)
        for field, ref in enumerate((u_ref, v_ref)):
            value = select(ref, first)
            if field == 0:
                own_ref[:, here] = value
            for part in range(parts):
                lane = slice(part * lanes, (part + 1) * lanes)
                pair_ref[part, :, field, here] = value[:apart, :, lane]
            if half_refs:
                rest[...] = value[apart:]
            for mask, half_ref in enumerate(half_refs):
                start = pl.multiple_of((spot_ref[0] ^ mask) * lanes, lanes)
                half_ref[:, field, here] = rest[:, :, pl.ds(start, lanes)]
        return carry

    lax.fori_loop(0, rows // ROWS, some, 0)


def pack(counts, spot, u, v, apart, kept, near):
    rows, planes, width = u.shape
    lanes = unit_lanes(width)
    parts = width // lanes
    group = step_rows(rows)
    others = kept - apart
    halves = near if others > 0 else 0
    return pl.pallas_call(
        pack_kernel,
        grid=(rows // group,),
        out_shape=[
            jax.ShapeDtypeStruct((kept, rows, width), jnp.bfloat16),
            jax.ShapeDtypeStruct((parts, apart, 2, rows, lanes), jnp.bfloat16),
        ]
        + [jax.ShapeDtypeStruct((others, 2, rows, lanes), jnp.bfloat16)] * halves,
        in_specs=[
            pl.BlockSpec(memory_space=pltpu.SMEM),
            pl.BlockSpec(memory_space=pltpu.SMEM),
            pl.BlockSpec((group, planes, width), lambda i: (i, 0, 0)),
            pl.BlockSpec((group, planes, width), lambda i: (i, 0, 0)),
        ],
        out_specs=[
            pl.BlockSpec((kept, group, width), lambda i: (0, i, 0)),
            pl.BlockSpec((parts, apart, 2, group, lanes), lambda i: (0, 0, 0, i, 0)),
        ]
        + [pl.BlockSpec((others, 2, group, lanes), lambda i: (0, 0, i, 0))] * halves,
        scratch_shapes=[
            pltpu.SMEM((planes,), jnp.int32),
            pltpu.VMEM((kept * HALF, HALF * planes), jnp.bfloat16),
            pltpu.VMEM((max(others, 1), ROWS, width), jnp.bfloat16),
        ],
        compiler_params=params(1),
        cost_estimate=NO_COST,
        name="pack",
    )(counts, spot, u, v)


def band_rows(matrix_ref, coef_ref, order, rows, planes):
    taps = coef_ref.shape[1]
    span = rows * planes
    spread = (2 * rows, span)
    row = lax.broadcasted_iota(jnp.int32, spread, 0)
    later = row >= rows
    plane = lax.broadcasted_iota(jnp.int32, spread, 1) - planes * jnp.where(later, row - rows, row)
    inside = (plane >= 0) & (plane < planes)

    def one(pair, carry):
        slot = 2 * pair
        ahead = plane - jnp.where(later, order[slot + 1], order[slot]) + taps // 2
        ahead = jnp.where(ahead < 0, ahead + planes, ahead)
        ahead = jnp.where(ahead >= planes, ahead - planes, ahead)
        ahead = jnp.where(inside, ahead, -1)
        start = pl.multiple_of(slot * rows, 2 * rows)

        def tap(index, values):
            hit = ahead == index
            on_u, on_f = VISCOSITY * coef_ref[1, index], -coef_ref[0, index]
            return (
                values[0] + jnp.where(hit, on_u, 0.0),
                values[1] + jnp.where(hit, on_f, 0.0),
            )

        zero = jnp.zeros(spread, jnp.float32)
        for field, value in enumerate(lax.fori_loop(0, taps, tap, (zero, zero), unroll=True)):
            high = value.astype(jnp.bfloat16)
            low = (value - high.astype(jnp.float32)).astype(jnp.bfloat16)
            matrix_ref[0, pl.ds(start, 2 * rows), field * span : (field + 1) * span] = high
            matrix_ref[1, pl.ds(start, 2 * rows), field * span : (field + 1) * span] = low
        return carry

    lax.fori_loop(0, matrix_ref.shape[1] // (2 * rows), one, 0)


def span_kernel(counts_ref, coef_ref, u_ref, w_ref, out_ref, order, bands):
    rows, planes, width = u_ref.shape
    kept = out_ref.shape[0]

    @pl.when(pl.program_id(0) == 0)
    def _():
        list_fluid(counts_ref, order)
        band_rows(bands, coef_ref, order, HALF, planes)

    def some(index, carry):
        here = pl.ds(pl.multiple_of(index * HALF, HALF), HALF)
        u = u_ref[here].reshape(HALF * planes, width)
        w = w_ref[here].reshape(HALF * planes, width)
        flux = (u.astype(jnp.float32) * w.astype(jnp.float32)).astype(jnp.bfloat16)
        fields = jnp.concatenate([u, flux], axis=0)
        acc = jnp.dot(bands[0], fields, preferred_element_type=jnp.float32)
        acc = acc + jnp.dot(bands[1], fields, preferred_element_type=jnp.float32)
        out_ref[:, here] = acc.reshape(kept, HALF, width)
        return carry

    lax.fori_loop(0, rows // HALF, some, 0)


def span_terms(counts, coef, u, w, kept):
    rows, planes, width = u.shape
    group = step_rows(rows)
    return pl.pallas_call(
        span_kernel,
        grid=(rows // group,),
        out_shape=jax.ShapeDtypeStruct((kept, rows, width), jnp.float32),
        in_specs=[
            pl.BlockSpec(memory_space=pltpu.SMEM),
            pl.BlockSpec(memory_space=pltpu.SMEM),
            pl.BlockSpec((group, planes, width), lambda i: (i, 0, 0)),
            pl.BlockSpec((group, planes, width), lambda i: (i, 0, 0)),
        ],
        out_specs=pl.BlockSpec((kept, group, width), lambda i: (0, i, 0)),
        scratch_shapes=[
            pltpu.SMEM((planes,), jnp.int32),
            pltpu.VMEM((2, kept * HALF, 2 * HALF * planes), jnp.bfloat16),
        ],
        compiler_params=params(1),
        cost_estimate=NO_COST,
        name="span_terms",
    )(counts, coef, u, w)


def stream_kernel(spots_ref, *refs):
    *block_refs, first_ref, second_ref, span_ref, out_ref, matrix, both = refs
    group, rows, width = block_refs[0].shape
    own = first_ref.shape[0]
    places = len(block_refs)

    @pl.when(pl.program_id(0) == 0)
    def _():
        def prepare(place, carry):
            lane = pl.ds(pl.multiple_of(spots_ref[place] * width, width), width)

            def some(index, carry):
                row = pl.ds(pl.multiple_of(index * CHUNK, CHUNK), CHUNK)
                matrix[place, row, :width] = second_ref[row, lane] * jnp.bfloat16(VISCOSITY)
                matrix[place, row, width:] = -first_ref[row, lane]
                return carry

            return lax.fori_loop(0, own // CHUNK, some, carry)

        lax.fori_loop(0, places, prepare, 0)

    for place, ref in enumerate(block_refs):

        def square(slot, carry):
            u = ref[slot]
            full = u.astype(jnp.float32)
            row = pl.ds(pl.multiple_of(slot * rows, rows), rows)
            both[place, row, :width] = u
            both[place, row, width:] = (full * full).astype(jnp.bfloat16)
            return carry

        lax.fori_loop(0, group, square, 0)

    out_ref[...] = span_ref[...]

    def one(place, carry):
        part = lax.dot_general(
            both[place],
            matrix[place],
            (((1,), (1,)), ((), ())),
            preferred_element_type=jnp.float32,
        )
        out_ref[...] += part.reshape(out_ref.shape)
        return carry

    lax.fori_loop(0, places, one, 0)


def stream_terms(spots, blocks, first, second, span):
    kept, rows, width = blocks[0].shape
    own, total = first.shape
    group = min(4, kept)
    by_group = pl.BlockSpec((group, rows, width), lambda i: (i, 0, 0))
    whole = pl.BlockSpec((own, total), lambda i: (0, 0))
    return pl.pallas_call(
        stream_kernel,
        grid=(pl.cdiv(kept, group),),
        out_shape=jax.ShapeDtypeStruct((kept, rows, own), jnp.float32),
        in_specs=[pl.BlockSpec(memory_space=pltpu.SMEM)]
        + [by_group] * len(blocks)
        + [whole, whole, pl.BlockSpec((group, rows, own), lambda i: (i, 0, 0))],
        out_specs=pl.BlockSpec((group, rows, own), lambda i: (i, 0, 0)),
        scratch_shapes=[
            pltpu.VMEM((len(blocks), own, 2 * width), jnp.bfloat16),
            pltpu.VMEM((len(blocks), group * rows, 2 * width), jnp.bfloat16),
        ],
        compiler_params=params(1),
        cost_estimate=NO_COST,
        name="stream_terms",
    )(spots, *blocks, first, second, span)


def swap_rows(array, mask):
    count = lax.axis_size("row")
    return lax.ppermute(array, "row", [(row, row ^ mask) for row in range(count)])


def gather_rows(own, other):
    mask = lax.axis_size("row") // 2
    row = lax.axis_index("row")
    blocks, spots = [own, other], [row, row ^ mask]
    while mask > 1:
        mask //= 2
        blocks = blocks + [swap_rows(block, mask) for block in blocks]
        spots = spots + [spot ^ mask for spot in spots]
    return blocks, jnp.stack(spots).astype(jnp.int32)


def wall_kernel(whole_steps, spot_ref, matrix_ref, pair_ref, *refs):
    *half_refs, out_ref, lines = refs
    sources, group, _, rows, lanes = pair_ref.shape
    total = sources * rows
    step = pl.program_id(0)
    pack_units = 2 if group % 2 == 0 else 1

    def both(u, v):
        return u, (u.astype(jnp.float32) * v.astype(jnp.float32)).astype(jnp.bfloat16)

    def put(unit, terms):
        terms = terms.astype(jnp.bfloat16)
        for k in range(pack_units):
            lane = slice(k * lanes, (k + 1) * lanes)
            out_ref[:, unit + k] = terms[:, lane].reshape(sources, rows, lanes)

    @pl.when(step < whole_steps)
    def _():
        def some(index, carry):
            unit = index * pack_units
            for k in range(pack_units):
                u, flux = both(pair_ref[:, unit + k, 0], pair_ref[:, unit + k, 1])
                lane = slice(k * lanes, (k + 1) * lanes)
                lines[:total, lane] = u.reshape(total, lanes)
                lines[total:, lane] = flux.reshape(total, lanes)
            put(unit, jnp.dot(matrix_ref[...], lines[...], preferred_element_type=jnp.float32))
            return carry

        lax.fori_loop(0, group // pack_units, some, 0)

    if len(half_refs) == 0:
        return
    near = total // 2

    @pl.when(step >= whole_steps)
    def _():
        def some(index, carry):
            unit = index * pack_units
            for mask, ref in enumerate(half_refs):
                start = pl.multiple_of((spot_ref[0] ^ mask) * rows, rows)
                for k in range(pack_units):
                    u, flux = both(ref[unit + k, 0], ref[unit + k, 1])
                    lane = slice(k * lanes, (k + 1) * lanes)
                    lines[pl.ds(start, rows), lane] = u
                    lines[pl.ds(start + near, rows), lane] = flux
            on_u = pl.ds(pl.multiple_of(spot_ref[1] * near, near), near)
            on_flux = pl.ds(pl.multiple_of(total + spot_ref[1] * near, near), near)
            terms = jnp.dot(
                matrix_ref[:, on_u], lines[:near], preferred_element_type=jnp.float32
            ) + jnp.dot(
                matrix_ref[:, on_flux], lines[near : 2 * near], preferred_element_type=jnp.float32
            )
            put(unit, terms)
            return carry

        lax.fori_loop(0, group // pack_units, some, 0)


def wall_terms(spot, matrix, pairs, halves):
    sources, units, _, rows, lanes = pairs.shape
    more = halves[0].shape[0] if halves else 0
    group = next(g for g in (4, 6, 10, 2, 1) if units % g == 0)
    whole_steps = units // group
    pack_units = 2 if group % 2 == 0 else 1
    half_blocks = [
        pl.BlockSpec((group, 2, rows, lanes), lambda i: (jnp.maximum(i - whole_steps, 0), 0, 0, 0))
    ] * len(halves)
    return pl.pallas_call(
        functools.partial(wall_kernel, whole_steps),
        grid=(whole_steps + pl.cdiv(more, group),),
        out_shape=jax.ShapeDtypeStruct((sources, units + more, rows, lanes), jnp.bfloat16),
        in_specs=[
            pl.BlockSpec(memory_space=pltpu.SMEM),
            pl.BlockSpec(matrix.shape, lambda i: (0, 0)),
            pl.BlockSpec(
                (sources, group, 2, rows, lanes),
                lambda i: (0, jnp.minimum(i, whole_steps - 1), 0, 0, 0),
            ),
        ]
        + half_blocks,
        out_specs=pl.BlockSpec((sources, group, rows, lanes), lambda i: (0, i, 0, 0)),
        scratch_shapes=[pltpu.VMEM((2 * sources * rows, pack_units * lanes), jnp.bfloat16)],
        compiler_params=params(1),
        cost_estimate=NO_COST,
        name="wall_terms",
    )(spot, matrix, pairs, *halves)


def finish_kernel(apart, counts_ref, base_ref, wall_ref, out_ref, order, chosen, placed):
    rows, planes, width = out_ref.shape
    kept = base_ref.shape[0]
    places, units, _, lanes = wall_ref.shape
    parts = width // lanes
    whole = parts * apart // places

    @pl.when(pl.program_id(0) == 0)
    def _():
        found = list_fluid(counts_ref, order)
        one_hot_rows(chosen, order, HALF, planes, found)
        placed[...] = chosen[...].T

    def some(index, carry):
        here = pl.ds(pl.multiple_of(index * ROWS, ROWS), ROWS)
        columns = []
        for part in range(parts):
            first = part * places // parts
            pieces = [wall_ref[first + k, :whole, here] for k in range(places // parts)]
            column = jnp.concatenate(pieces, axis=0).astype(jnp.float32)
            if units > whole:
                low = wall_ref[part, whole:, here].astype(jnp.float32)
                high = wall_ref[part + parts, whole:, here].astype(jnp.float32)
                column = jnp.concatenate([column, low + high], axis=0)
            columns.append(column)
        value = base_ref[:, here] + jnp.concatenate(columns, axis=-1)
        for start in range(0, ROWS, HALF):
            some_rows = value[:, start : start + HALF].reshape(kept * HALF, width)
            out = jnp.dot(
                placed[...], some_rows.astype(jnp.bfloat16), preferred_element_type=jnp.float32
            )
            out_ref[pl.ds(index * ROWS + start, HALF)] = out.astype(jnp.bfloat16).reshape(
                HALF, planes, width
            )
        return carry

    lax.fori_loop(0, rows // ROWS, some, 0)


def finish(counts, base, wall, planes, apart):
    kept, rows, width = base.shape
    places, units, _, lanes = wall.shape
    group = step_rows(rows)
    return pl.pallas_call(
        functools.partial(finish_kernel, apart),
        grid=(rows // group,),
        out_shape=jax.ShapeDtypeStruct((rows, planes, width), jnp.bfloat16),
        in_specs=[
            pl.BlockSpec(memory_space=pltpu.SMEM),
            pl.BlockSpec((kept, group, width), lambda i: (0, i, 0)),
            pl.BlockSpec((places, units, group, lanes), lambda i: (0, 0, i, 0)),
        ],
        out_specs=pl.BlockSpec((group, planes, width), lambda i: (i, 0, 0)),
        scratch_shapes=[
            pltpu.SMEM((planes,), jnp.int32),
            pltpu.VMEM((kept * HALF, HALF * planes), jnp.bfloat16),
            pltpu.VMEM((HALF * planes, kept * HALF), jnp.bfloat16),
        ],
        compiler_params=params(1),
        cost_estimate=NO_COST,
        name="finish",
    )(counts, base, wall)


def swap(array, mask):
    count = lax.axis_size("col")
    if mask == 0:
        return array
    return lax.ppermute(array, "col", [(column, column ^ mask) for column in range(count)])


def with_kept(
    apart, kept, u, v, w, first, second, wall_first, wall_second, metric1, metric2, coef, counts
):
    rows, planes, width = u.shape
    columns = lax.axis_size("col")
    column = lax.axis_index("col")
    near = columns // 2
    spot = jnp.stack([column % near, column // near]).astype(jnp.int32)
    own, pairs, *halves = pack(counts, spot, u, v, apart, kept, near)
    parts, _, _, _, lanes = pairs.shape
    units = parts * apart // columns
    lines = lax.all_to_all(
        pairs.reshape(columns, units, 2, rows, lanes), "col", split_axis=0, concat_axis=0
    )
    halves = [swap(half, mask) for mask, half in enumerate(halves)]
    one, two = metric1[:, None], metric2[:, None]
    wide_first = wall_first.astype(jnp.float32)
    on_stream = VISCOSITY * (one * one * wall_second.astype(jnp.float32) + two * wide_first)
    matrix = jnp.concatenate([on_stream, -one * wide_first], axis=1).astype(jnp.bfloat16)
    first_block = swap_rows(own, lax.axis_size("row") // 2)
    lines, halves, first_block = lax.optimization_barrier((lines, halves, first_block))
    wall = wall_terms(spot, matrix, lines, halves)
    wall = lax.all_to_all(wall, "col", split_axis=0, concat_axis=0)
    blocks, spots = gather_rows(own, first_block)
    span = span_terms(counts, coef, u, w, kept)
    base = stream_terms(spots, blocks, first, second, span)
    return finish(counts, base, wall, planes, apart)


def share_of(kept, parts, columns):
    if 2 * parts != columns:
        return kept
    options = range(columns // 2, kept + 1, columns // 2)
    return min(options, key=lambda a: max(2 * a, 1.5 * a + kept - a) + a + 2 * (kept - a))


def on_device(u, v, w, first, second, wall_first, wall_second, metric1, metric2, coef, counts):
    u, v, w = (jnp.swapaxes(t, 1, 2) for t in (u, v, w))
    planes, width = u.shape[1:]
    columns = lax.axis_size("col")
    parts = width // unit_lanes(width)
    step = 2 if 2 * parts == columns else columns // math.gcd(columns, parts)
    blocks = counts.shape[0]
    least, middle = blocks - 1 + ZB, (blocks - 1) * (ZB + 1) / 2 + ZB
    sizes = [size for size in range(step, planes, step) if size >= least]
    sizes = [size for size in sizes if abs(size - middle) < 3.5 * step] + [planes]
    branches = [
        functools.partial(with_kept, share_of(size, parts, columns), size) for size in sizes
    ]
    fluid = jnp.sum(counts)
    index = (fluid - sizes[0] + (step - 1)) // step
    operands = (u, v, w, first, second, wall_first, wall_second, metric1, metric2, coef, counts)
    out = lax.switch(index, branches, *operands)
    return jnp.swapaxes(out, 1, 2)


def solution(mesh):
    field = P("col", "row", None)
    placed = (field, field, field, P("row", None), P("row", None)) + (P(),) * 6
    return jax.shard_map(
        on_device,
        mesh=mesh,
        in_specs=placed,
        out_specs=field,
        check_vma=False,
    )
```

```python
import functools
import math

import jax
import jax.numpy as jnp
from jax import lax
from jax.experimental import pallas as pl
from jax.experimental.pallas import tpu as pltpu
from jax.sharding import PartitionSpec as P

ZB = 4
LANES = 128
ROWS = 16
HALF = 8
CHUNK = 32
VISCOSITY = 0.25
VMEM_BYTES = 63 * 1024 * 1024
NO_COST = pl.CostEstimate(flops=0, bytes_accessed=0, transcendentals=0)
HIGH_COST = pl.CostEstimate(flops=10**12, bytes_accessed=10**9, transcendentals=0)


def params(steps):
    return pltpu.CompilerParams(
        dimension_semantics=("arbitrary",) * steps, vmem_limit_bytes=VMEM_BYTES
    )


def unit_lanes(width):
    return LANES if width % LANES == 0 else width


def even(kept):
    return kept + kept % 2


def step_rows(rows):
    return next(g for g in (2 * ROWS, ROWS, rows) if rows % g == 0)


def list_fluid(counts_ref, order_ref):
    planes = order_ref.shape[0]

    def clear(plane, carry):
        order_ref[plane] = 0
        return carry

    lax.fori_loop(0, planes, clear, 0)

    def visit(plane, filled):
        fluid = lax.rem(plane, ZB) < counts_ref[plane // ZB]

        @pl.when(fluid)
        def _():
            order_ref[filled] = plane

        return filled + fluid.astype(jnp.int32)

    return lax.fori_loop(0, planes, visit, 0)


def one_hot_rows(matrix_ref, order, rows, planes, found):
    spread = (2 * rows, rows * planes)
    row = lax.broadcasted_iota(jnp.int32, spread, 0)
    later = row >= rows
    near = lax.broadcasted_iota(jnp.int32, spread, 1) - planes * jnp.where(later, row - rows, row)

    def one(pair, carry):
        slot = 2 * pair
        here = jnp.where(slot < found, order[slot], -rows * planes)
        after = jnp.where(slot + 1 < found, order[slot + 1], -rows * planes)
        hot = jnp.where(near == jnp.where(later, after, here), 1.0, 0.0).astype(jnp.bfloat16)
        start = pl.multiple_of(slot * rows, 2 * rows)
        matrix_ref[pl.ds(start, 2 * rows), :] = hot
        return carry

    lax.fori_loop(0, matrix_ref.shape[0] // (2 * rows), one, 0)


def pack_kernel(counts_ref, spot_ref, u_ref, v_ref, own_ref, pair_ref, *refs):
    *half_refs, order, chosen, rest = refs
    rows, planes, width = u_ref.shape
    kept = own_ref.shape[0]
    parts, apart, _, _, lanes = pair_ref.shape

    @pl.when(pl.program_id(0) == 0)
    def _():
        found = list_fluid(counts_ref, order)
        one_hot_rows(chosen, order, HALF, planes, found)

    def select(ref, first):
        picked = []
        for start in range(0, ROWS, HALF):
            flat = ref[pl.ds(first + start, HALF)].reshape(HALF * planes, width)
            part = jnp.dot(chosen[...], flat, preferred_element_type=jnp.float32)
            picked.append(part.reshape(-1, HALF, width)[:kept])
        return jnp.concatenate(picked, axis=1).astype(jnp.bfloat16)

    def some(index, carry):
        first = pl.multiple_of(index * ROWS, ROWS)
        here = pl.ds(first, ROWS)
        for field, ref in enumerate((u_ref, v_ref)):
            value = select(ref, first)
            if field == 0:
                own_ref[:, here] = value
            for part in range(parts):
                lane = slice(part * lanes, (part + 1) * lanes)
                pair_ref[part, :, field, here] = value[:apart, :, lane]
            if half_refs:
                rest[...] = value[apart:]
            for mask, half_ref in enumerate(half_refs):
                start = pl.multiple_of((spot_ref[0] ^ mask) * lanes, lanes)
                half_ref[:, field, here] = rest[:, :, pl.ds(start, lanes)]
        return carry

    lax.fori_loop(0, rows // ROWS, some, 0)


def pack(counts, spot, u, v, apart, kept, near):
    rows, planes, width = u.shape
    lanes = unit_lanes(width)
    parts = width // lanes
    group = step_rows(rows)
    others = kept - apart
    halves = near if others > 0 else 0
    return pl.pallas_call(
        pack_kernel,
        grid=(rows // group,),
        out_shape=[
            jax.ShapeDtypeStruct((kept, rows, width), jnp.bfloat16),
            jax.ShapeDtypeStruct((parts, apart, 2, rows, lanes), jnp.bfloat16),
        ]
        + [jax.ShapeDtypeStruct((others, 2, rows, lanes), jnp.bfloat16)] * halves,
        in_specs=[
            pl.BlockSpec(memory_space=pltpu.SMEM),
            pl.BlockSpec(memory_space=pltpu.SMEM),
            pl.BlockSpec((group, planes, width), lambda i: (i, 0, 0)),
            pl.BlockSpec((group, planes, width), lambda i: (i, 0, 0)),
        ],
        out_specs=[
            pl.BlockSpec((kept, group, width), lambda i: (0, i, 0)),
            pl.BlockSpec((parts, apart, 2, group, lanes), lambda i: (0, 0, 0, i, 0)),
        ]
        + [pl.BlockSpec((others, 2, group, lanes), lambda i: (0, 0, i, 0))] * halves,
        scratch_shapes=[
            pltpu.SMEM((planes,), jnp.int32),
            pltpu.VMEM((even(kept) * HALF, HALF * planes), jnp.bfloat16),
            pltpu.VMEM((max(others, 1), ROWS, width), jnp.bfloat16),
        ],
        compiler_params=params(1),
        cost_estimate=NO_COST,
        name="pack",
    )(counts, spot, u, v)


def band_rows(matrix_ref, coef_ref, order, rows, planes):
    taps = coef_ref.shape[1]
    span = rows * planes
    spread = (2 * rows, span)
    row = lax.broadcasted_iota(jnp.int32, spread, 0)
    later = row >= rows
    plane = lax.broadcasted_iota(jnp.int32, spread, 1) - planes * jnp.where(later, row - rows, row)
    inside = (plane >= 0) & (plane < planes)

    def one(pair, carry):
        slot = 2 * pair
        ahead = plane - jnp.where(later, order[slot + 1], order[slot]) + taps // 2
        ahead = jnp.where(ahead < 0, ahead + planes, ahead)
        ahead = jnp.where(ahead >= planes, ahead - planes, ahead)
        ahead = jnp.where(inside, ahead, -1)
        start = pl.multiple_of(slot * rows, 2 * rows)

        def tap(index, values):
            hit = ahead == index
            on_u, on_f = VISCOSITY * coef_ref[1, index], -coef_ref[0, index]
            return (
                values[0] + jnp.where(hit, on_u, 0.0),
                values[1] + jnp.where(hit, on_f, 0.0),
            )

        zero = jnp.zeros(spread, jnp.float32)
        for field, value in enumerate(lax.fori_loop(0, taps, tap, (zero, zero), unroll=True)):
            high = value.astype(jnp.bfloat16)
            low = (value - high.astype(jnp.float32)).astype(jnp.bfloat16)
            matrix_ref[0, pl.ds(start, 2 * rows), field * span : (field + 1) * span] = high
            matrix_ref[1, pl.ds(start, 2 * rows), field * span : (field + 1) * span] = low
        return carry

    lax.fori_loop(0, matrix_ref.shape[1] // (2 * rows), one, 0)


def span_kernel(counts_ref, coef_ref, u_ref, w_ref, out_ref, order, bands):
    rows, planes, width = u_ref.shape
    kept = out_ref.shape[0]

    @pl.when(pl.program_id(0) == 0)
    def _():
        list_fluid(counts_ref, order)
        band_rows(bands, coef_ref, order, HALF, planes)

    def some(index, carry):
        here = pl.ds(pl.multiple_of(index * HALF, HALF), HALF)
        u = u_ref[here].reshape(HALF * planes, width)
        w = w_ref[here].reshape(HALF * planes, width)
        flux = (u.astype(jnp.float32) * w.astype(jnp.float32)).astype(jnp.bfloat16)
        fields = jnp.concatenate([u, flux], axis=0)
        acc = jnp.dot(bands[0], fields, preferred_element_type=jnp.float32)
        acc = acc + jnp.dot(bands[1], fields, preferred_element_type=jnp.float32)
        out_ref[:, here] = acc.reshape(-1, HALF, width)[:kept]
        return carry

    lax.fori_loop(0, rows // HALF, some, 0)


def span_terms(counts, coef, u, w, kept):
    rows, planes, width = u.shape
    group = step_rows(rows)
    return pl.pallas_call(
        span_kernel,
        grid=(rows // group,),
        out_shape=jax.ShapeDtypeStruct((kept, rows, width), jnp.float32),
        in_specs=[
            pl.BlockSpec(memory_space=pltpu.SMEM),
            pl.BlockSpec(memory_space=pltpu.SMEM),
            pl.BlockSpec((group, planes, width), lambda i: (i, 0, 0)),
            pl.BlockSpec((group, planes, width), lambda i: (i, 0, 0)),
        ],
        out_specs=pl.BlockSpec((kept, group, width), lambda i: (0, i, 0)),
        scratch_shapes=[
            pltpu.SMEM((planes,), jnp.int32),
            pltpu.VMEM((2, even(kept) * HALF, 2 * HALF * planes), jnp.bfloat16),
        ],
        compiler_params=params(1),
        cost_estimate=NO_COST,
        name="span_terms",
    )(counts, coef, u, w)


def stream_kernel(spots_ref, *refs):
    *block_refs, first_ref, second_ref, span_ref, out_ref, matrix, both = refs
    group, rows, width = block_refs[0].shape
    own = first_ref.shape[0]
    places = len(block_refs)

    @pl.when(pl.program_id(0) == 0)
    def _():
        def prepare(place, carry):
            lane = pl.ds(pl.multiple_of(spots_ref[place] * width, width), width)

            def some(index, carry):
                row = pl.ds(pl.multiple_of(index * CHUNK, CHUNK), CHUNK)
                matrix[place, row, :width] = second_ref[row, lane] * jnp.bfloat16(VISCOSITY)
                matrix[place, row, width:] = -first_ref[row, lane]
                return carry

            return lax.fori_loop(0, own // CHUNK, some, carry)

        lax.fori_loop(0, places, prepare, 0)

    for place, ref in enumerate(block_refs):

        def square(slot, carry):
            u = ref[slot]
            full = u.astype(jnp.float32)
            row = pl.ds(pl.multiple_of(slot * rows, rows), rows)
            both[place, row, :width] = u
            both[place, row, width:] = (full * full).astype(jnp.bfloat16)
            return carry

        lax.fori_loop(0, group, square, 0)

    out_ref[...] = span_ref[...]

    def one(place, carry):
        part = lax.dot_general(
            both[place],
            matrix[place],
            (((1,), (1,)), ((), ())),
            preferred_element_type=jnp.float32,
        )
        out_ref[...] += part.reshape(out_ref.shape)
        return carry

    lax.fori_loop(0, places, one, 0)


def stream_terms(spots, blocks, first, second, span):
    kept, rows, width = blocks[0].shape
    own, total = first.shape
    group = min(4, kept)
    by_group = pl.BlockSpec((group, rows, width), lambda i: (i, 0, 0))
    whole = pl.BlockSpec((own, total), lambda i: (0, 0))
    return pl.pallas_call(
        stream_kernel,
        grid=(pl.cdiv(kept, group),),
        out_shape=jax.ShapeDtypeStruct((kept, rows, own), jnp.float32),
        in_specs=[pl.BlockSpec(memory_space=pltpu.SMEM)]
        + [by_group] * len(blocks)
        + [whole, whole, pl.BlockSpec((group, rows, own), lambda i: (i, 0, 0))],
        out_specs=pl.BlockSpec((group, rows, own), lambda i: (i, 0, 0)),
        scratch_shapes=[
            pltpu.VMEM((len(blocks), own, 2 * width), jnp.bfloat16),
            pltpu.VMEM((len(blocks), group * rows, 2 * width), jnp.bfloat16),
        ],
        compiler_params=params(1),
        cost_estimate=NO_COST,
        name="stream_terms",
    )(spots, *blocks, first, second, span)


def swap_rows(array, mask):
    count = lax.axis_size("row")
    return lax.ppermute(array, "row", [(row, row ^ mask) for row in range(count)])


def gather_rows(own, other):
    mask = lax.axis_size("row") // 2
    row = lax.axis_index("row")
    blocks, spots = [own, other], [row, row ^ mask]
    while mask > 1:
        mask //= 2
        blocks = blocks + [swap_rows(block, mask) for block in blocks]
        spots = spots + [spot ^ mask for spot in spots]
    return blocks, jnp.stack(spots).astype(jnp.int32)


def with_flux(pair):
    u, v = pair
    return u, (u.astype(jnp.float32) * v.astype(jnp.float32)).astype(jnp.bfloat16)


def abreast(group):
    return 2 if group % 2 == 0 else 1


def units_a_step(units):
    return next(g for g in (4, 6, 10, 2, 1) if units % g == 0)


def whole_kernel(matrix_ref, pair_ref, _, out_ref, lines):
    sources, group, _, rows, lanes = pair_ref.shape
    total = sources * rows
    side = abreast(group)

    def some(index, carry):
        for k in range(side):
            unit = index * side + k
            lane = slice(k * lanes, (k + 1) * lanes)
            u, flux = with_flux((pair_ref[:, unit, 0], pair_ref[:, unit, 1]))
            lines[:total, lane] = u.reshape(total, lanes)
            lines[total:, lane] = flux.reshape(total, lanes)
        terms = jnp.dot(matrix_ref[...], lines[...], preferred_element_type=jnp.float32)
        terms = terms.astype(jnp.bfloat16)
        for k in range(side):
            lane = slice(k * lanes, (k + 1) * lanes)
            out_ref[:, index * side + k] = terms[:, lane].reshape(sources, rows, lanes)
        return carry

    lax.fori_loop(0, group // side, some, 0)


def whole_terms(matrix, pairs, behind):
    sources, units, _, rows, lanes = pairs.shape
    group = units_a_step(units)
    return pl.pallas_call(
        whole_kernel,
        grid=(units // group,),
        out_shape=jax.ShapeDtypeStruct(behind.shape, behind.dtype),
        in_specs=[
            pl.BlockSpec(matrix.shape, lambda i: (0, 0)),
            pl.BlockSpec((sources, group, 2, rows, lanes), lambda i: (0, i, 0, 0, 0)),
            pl.BlockSpec(memory_space=pl.ANY),
        ],
        out_specs=pl.BlockSpec((sources, group, rows, lanes), lambda i: (0, i, 0, 0)),
        scratch_shapes=[pltpu.VMEM((2 * sources * rows, abreast(group) * lanes), jnp.bfloat16)],
        input_output_aliases={2: 0},
        compiler_params=params(1),
        cost_estimate=NO_COST,
        name="whole_terms",
    )(matrix, pairs, behind)


def half_kernel(spot_ref, matrix_ref, *refs):
    *pair_refs, out_ref, lines = refs
    group, _, rows, lanes = pair_refs[0].shape
    side = abreast(group)
    half = len(pair_refs) * rows
    on_u = pl.ds(pl.multiple_of(spot_ref[1] * half, half), half)
    on_flux = pl.ds(pl.multiple_of((2 + spot_ref[1]) * half, half), half)

    def some(index, carry):
        for mask, ref in enumerate(pair_refs):
            start = pl.multiple_of((spot_ref[0] ^ mask) * rows, rows)
            for k in range(side):
                unit = index * side + k
                lane = slice(k * lanes, (k + 1) * lanes)
                u, flux = with_flux((ref[unit, 0], ref[unit, 1]))
                lines[pl.ds(start, rows), lane] = u
                lines[pl.ds(pl.multiple_of(half + start, rows), rows), lane] = flux
        terms = jnp.dot(matrix_ref[:, on_u], lines[:half], preferred_element_type=jnp.float32)
        terms = terms + jnp.dot(
            matrix_ref[:, on_flux], lines[half:], preferred_element_type=jnp.float32
        )
        terms = terms.astype(jnp.bfloat16)
        for k in range(side):
            lane = slice(k * lanes, (k + 1) * lanes)
            out_ref[:, index * side + k] = terms[:, lane].reshape(-1, rows, lanes)
        return carry

    lax.fori_loop(0, group // side, some, 0)


def half_terms(spot, matrix, pairs, before):
    near = len(pairs)
    units, _, rows, lanes = pairs[0].shape
    group = units_a_step(before)
    side = abreast(group)
    return pl.pallas_call(
        half_kernel,
        grid=(pl.cdiv(units, group),),
        out_shape=jax.ShapeDtypeStruct((2 * near, before + units, rows, lanes), jnp.bfloat16),
        in_specs=[
            pl.BlockSpec(memory_space=pltpu.SMEM),
            pl.BlockSpec(matrix.shape, lambda i: (0, 0)),
        ]
        + [pl.BlockSpec((group, 2, rows, lanes), lambda i: (i, 0, 0, 0))] * near,
        out_specs=pl.BlockSpec(
            (2 * near, group, rows, lanes), lambda i: (0, before // group + i, 0, 0)
        ),
        scratch_shapes=[pltpu.VMEM((2 * near * rows, side * lanes), jnp.bfloat16)],
        compiler_params=params(1),
        cost_estimate=HIGH_COST,
        name="half_terms",
    )(spot, matrix, *pairs)


def finish_kernel(apart, counts_ref, base_ref, wall_ref, out_ref, order, chosen, placed):
    rows, planes, width = out_ref.shape
    kept = base_ref.shape[0]
    places, units, _, lanes = wall_ref.shape
    parts = width // lanes
    whole = parts * apart // places

    @pl.when(pl.program_id(0) == 0)
    def _():
        found = list_fluid(counts_ref, order)
        one_hot_rows(chosen, order, HALF, planes, found)
        placed[...] = chosen[...].T

    def some(index, carry):
        here = pl.ds(pl.multiple_of(index * ROWS, ROWS), ROWS)
        columns = []
        for part in range(parts):
            first = part * places // parts
            pieces = [wall_ref[first + k, :whole, here] for k in range(places // parts)]
            column = jnp.concatenate(pieces, axis=0).astype(jnp.float32)
            if units > whole:
                low = wall_ref[part, whole:, here].astype(jnp.float32)
                high = wall_ref[part + parts, whole:, here].astype(jnp.float32)
                column = jnp.concatenate([column, low + high], axis=0)
            columns.append(column)
        value = base_ref[:, here] + jnp.concatenate(columns, axis=-1)
        if kept % 2 == 1:
            value = jnp.concatenate([value, jnp.zeros((1, ROWS, width), jnp.float32)], axis=0)
        for start in range(0, ROWS, HALF):
            some_rows = value[:, start : start + HALF].reshape(-1, width)
            out = jnp.dot(
                placed[...], some_rows.astype(jnp.bfloat16), preferred_element_type=jnp.float32
            )
            out_ref[pl.ds(index * ROWS + start, HALF)] = out.astype(jnp.bfloat16).reshape(
                HALF, planes, width
            )
        return carry

    lax.fori_loop(0, rows // ROWS, some, 0)


def finish(counts, base, wall, planes, apart):
    kept, rows, width = base.shape
    places, units, _, lanes = wall.shape
    group = step_rows(rows)
    return pl.pallas_call(
        functools.partial(finish_kernel, apart),
        grid=(rows // group,),
        out_shape=jax.ShapeDtypeStruct((rows, planes, width), jnp.bfloat16),
        in_specs=[
            pl.BlockSpec(memory_space=pltpu.SMEM),
            pl.BlockSpec((kept, group, width), lambda i: (0, i, 0)),
            pl.BlockSpec((places, units, group, lanes), lambda i: (0, 0, i, 0)),
        ],
        out_specs=pl.BlockSpec((group, planes, width), lambda i: (i, 0, 0)),
        scratch_shapes=[
            pltpu.SMEM((planes,), jnp.int32),
            pltpu.VMEM((even(kept) * HALF, HALF * planes), jnp.bfloat16),
            pltpu.VMEM((HALF * planes, even(kept) * HALF), jnp.bfloat16),
        ],
        compiler_params=params(1),
        cost_estimate=NO_COST,
        name="finish",
    )(counts, base, wall)


def swap(array, mask):
    count = lax.axis_size("col")
    if mask == 0:
        return array
    return lax.ppermute(array, "col", [(column, column ^ mask) for column in range(count)])


def with_kept(
    apart, kept, u, v, w, first, second, wall_first, wall_second, metric1, metric2, coef, counts
):
    rows, planes, width = u.shape
    columns = lax.axis_size("col")
    column = lax.axis_index("col")
    near = columns // 2
    spot = jnp.stack([column % near, column // near]).astype(jnp.int32)
    own, pairs, *halves = pack(counts, spot, u, v, apart, kept, near)
    parts, _, _, _, lanes = pairs.shape
    units = parts * apart // columns
    halves = [swap(half, mask) for mask, half in enumerate(halves)]
    if halves:
        pairs, halves[1] = lax.optimization_barrier((pairs, halves[1]))
    lines = lax.all_to_all(
        pairs.reshape(columns, units, 2, rows, lanes), "col", split_axis=0, concat_axis=0
    )
    one, two = metric1[:, None], metric2[:, None]
    wide_first = wall_first.astype(jnp.float32)
    on_stream = VISCOSITY * (one * one * wall_second.astype(jnp.float32) + two * wide_first)
    matrix = jnp.concatenate([on_stream, -one * wide_first], axis=1).astype(jnp.bfloat16)
    first_block = swap_rows(own, lax.axis_size("row") // 2)
    if halves:
        wall = half_terms(spot, matrix, halves, units)
    else:
        wall = jnp.zeros((columns, units, rows, lanes), jnp.bfloat16)
    lines, wall, first_block = lax.optimization_barrier((lines, wall, first_block))
    wall = whole_terms(matrix, lines, wall)
    wall = lax.all_to_all(wall, "col", split_axis=0, concat_axis=0)
    blocks, spots = gather_rows(own, first_block)
    span = span_terms(counts, coef, u, w, kept)
    base = stream_terms(spots, blocks, first, second, span)
    return finish(counts, base, wall, planes, apart)


def share_of(kept, parts, columns):
    if 2 * parts != columns:
        return kept
    options = range(columns // 2, kept + 1, columns // 2)
    return min(options, key=lambda a: max(12 + 2 * a, 2 + kept + a / 2) - 1.01 * a)


def on_device(u, v, w, first, second, wall_first, wall_second, metric1, metric2, coef, counts):
    u, v, w = (jnp.swapaxes(t, 1, 2) for t in (u, v, w))
    planes, width = u.shape[1:]
    columns = lax.axis_size("col")
    parts = width // unit_lanes(width)
    step = 1 if 2 * parts == columns else columns // math.gcd(columns, parts)
    blocks = counts.shape[0]
    least, middle = blocks - 1 + ZB, (blocks - 1) * (ZB + 1) / 2 + ZB
    sizes = [size for size in range(step, planes, step) if size >= least]
    sizes = [size for size in sizes if -4 < (size - middle) / step < 6] + [planes]
    branches = [
        functools.partial(with_kept, share_of(size, parts, columns), size) for size in sizes
    ]
    fluid = jnp.sum(counts)
    index = (fluid - sizes[0] + (step - 1)) // step
    operands = (u, v, w, first, second, wall_first, wall_second, metric1, metric2, coef, counts)
    out = lax.switch(index, branches, *operands)
    return jnp.swapaxes(out, 1, 2)


def solution(mesh):
    field = P("col", "row", None)
    placed = (field, field, field, P("row", None), P("row", None)) + (P(),) * 6
    return jax.shard_map(
        on_device,
        mesh=mesh,
        in_specs=placed,
        out_specs=field,
        check_vma=False,
    )
```

```python
import functools
import math

import jax
import jax.numpy as jnp
from jax import lax
from jax.experimental import pallas as pl
from jax.experimental.pallas import tpu as pltpu
from jax.sharding import PartitionSpec as P

ZB = 4
LANES = 128
ROWS = 16
HALF = 8
CHUNK = 32
VISCOSITY = 0.25
VMEM_BYTES = 63 * 1024 * 1024
NO_COST = pl.CostEstimate(flops=0, bytes_accessed=0, transcendentals=0)
HIGH_COST = pl.CostEstimate(flops=10**12, bytes_accessed=10**9, transcendentals=0)


def params(steps):
    return pltpu.CompilerParams(
        dimension_semantics=("arbitrary",) * steps, vmem_limit_bytes=VMEM_BYTES
    )


def unit_lanes(width):
    return LANES if width % LANES == 0 else width


def even(kept):
    return kept + kept % 2


def step_rows(rows):
    return next(g for g in (2 * ROWS, ROWS, rows) if rows % g == 0)


def list_fluid(counts_ref, order_ref):
    planes = order_ref.shape[0]

    def clear(plane, carry):
        order_ref[plane] = 0
        return carry

    lax.fori_loop(0, planes, clear, 0)

    def visit(plane, filled):
        fluid = lax.rem(plane, ZB) < counts_ref[plane // ZB]

        @pl.when(fluid)
        def _():
            order_ref[filled] = plane

        return filled + fluid.astype(jnp.int32)

    return lax.fori_loop(0, planes, visit, 0)


def one_hot_rows(matrix_ref, order, rows, planes, found):
    spread = (2 * rows, rows * planes)
    row = lax.broadcasted_iota(jnp.int32, spread, 0)
    later = row >= rows
    near = lax.broadcasted_iota(jnp.int32, spread, 1) - planes * jnp.where(later, row - rows, row)

    def one(pair, carry):
        slot = 2 * pair
        here = jnp.where(slot < found, order[slot], -rows * planes)
        after = jnp.where(slot + 1 < found, order[slot + 1], -rows * planes)
        hot = jnp.where(near == jnp.where(later, after, here), 1.0, 0.0).astype(jnp.bfloat16)
        start = pl.multiple_of(slot * rows, 2 * rows)
        matrix_ref[pl.ds(start, 2 * rows), :] = hot
        return carry

    lax.fori_loop(0, matrix_ref.shape[0] // (2 * rows), one, 0)


def pack_kernel(counts_ref, spot_ref, u_ref, v_ref, own_ref, pair_ref, *refs):
    *half_refs, order, chosen, rest = refs
    rows, planes, width = u_ref.shape
    kept = own_ref.shape[0]
    parts, apart, _, _, lanes = pair_ref.shape

    @pl.when(pl.program_id(0) == 0)
    def _():
        found = list_fluid(counts_ref, order)
        one_hot_rows(chosen, order, HALF, planes, found)

    def select(ref, first):
        picked = []
        for start in range(0, ROWS, HALF):
            flat = ref[pl.ds(first + start, HALF)].reshape(HALF * planes, width)
            part = jnp.dot(chosen[...], flat, preferred_element_type=jnp.float32)
            picked.append(part.reshape(-1, HALF, width)[:kept])
        return jnp.concatenate(picked, axis=1).astype(jnp.bfloat16)

    def some(index, carry):
        first = pl.multiple_of(index * ROWS, ROWS)
        here = pl.ds(first, ROWS)
        for field, ref in enumerate((u_ref, v_ref)):
            value = select(ref, first)
            if field == 0:
                own_ref[:, here] = value
            for part in range(parts):
                lane = slice(part * lanes, (part + 1) * lanes)
                pair_ref[part, :, field, here] = value[:apart, :, lane]
            if half_refs:
                rest[...] = value[apart:]
            for mask, half_ref in enumerate(half_refs):
                start = pl.multiple_of((spot_ref[0] ^ mask) * lanes, lanes)
                half_ref[:, field, here] = rest[:, :, pl.ds(start, lanes)]
        return carry

    lax.fori_loop(0, rows // ROWS, some, 0)


def pack(counts, spot, u, v, apart, kept, near):
    rows, planes, width = u.shape
    lanes = unit_lanes(width)
    parts = width // lanes
    group = step_rows(rows)
    others = kept - apart
    halves = near if others > 0 else 0
    return pl.pallas_call(
        pack_kernel,
        grid=(rows // group,),
        out_shape=[
            jax.ShapeDtypeStruct((kept, rows, width), jnp.bfloat16),
            jax.ShapeDtypeStruct((parts, apart, 2, rows, lanes), jnp.bfloat16),
        ]
        + [jax.ShapeDtypeStruct((others, 2, rows, lanes), jnp.bfloat16)] * halves,
        in_specs=[
            pl.BlockSpec(memory_space=pltpu.SMEM),
            pl.BlockSpec(memory_space=pltpu.SMEM),
            pl.BlockSpec((group, planes, width), lambda i: (i, 0, 0)),
            pl.BlockSpec((group, planes, width), lambda i: (i, 0, 0)),
        ],
        out_specs=[
            pl.BlockSpec((kept, group, width), lambda i: (0, i, 0)),
            pl.BlockSpec((parts, apart, 2, group, lanes), lambda i: (0, 0, 0, i, 0)),
        ]
        + [pl.BlockSpec((others, 2, group, lanes), lambda i: (0, 0, i, 0))] * halves,
        scratch_shapes=[
            pltpu.SMEM((planes,), jnp.int32),
            pltpu.VMEM((even(kept) * HALF, HALF * planes), jnp.bfloat16),
            pltpu.VMEM((max(others, 1), ROWS, width), jnp.bfloat16),
        ],
        compiler_params=params(1),
        cost_estimate=NO_COST,
        name="pack",
    )(counts, spot, u, v)


def band_rows(matrix_ref, coef_ref, order, rows, planes):
    taps = coef_ref.shape[1]
    span = rows * planes
    spread = (2 * rows, span)
    row = lax.broadcasted_iota(jnp.int32, spread, 0)
    later = row >= rows
    plane = lax.broadcasted_iota(jnp.int32, spread, 1) - planes * jnp.where(later, row - rows, row)
    inside = (plane >= 0) & (plane < planes)

    def one(pair, carry):
        slot = 2 * pair
        ahead = plane - jnp.where(later, order[slot + 1], order[slot]) + taps // 2
        ahead = jnp.where(ahead < 0, ahead + planes, ahead)
        ahead = jnp.where(ahead >= planes, ahead - planes, ahead)
        ahead = jnp.where(inside, ahead, -1)
        start = pl.multiple_of(slot * rows, 2 * rows)

        def tap(index, values):
            hit = ahead == index
            on_u, on_f = VISCOSITY * coef_ref[1, index], -coef_ref[0, index]
            return (
                values[0] + jnp.where(hit, on_u, 0.0),
                values[1] + jnp.where(hit, on_f, 0.0),
            )

        zero = jnp.zeros(spread, jnp.float32)
        for field, value in enumerate(lax.fori_loop(0, taps, tap, (zero, zero), unroll=True)):
            high = value.astype(jnp.bfloat16)
            low = (value - high.astype(jnp.float32)).astype(jnp.bfloat16)
            matrix_ref[0, pl.ds(start, 2 * rows), field * span : (field + 1) * span] = high
            matrix_ref[1, pl.ds(start, 2 * rows), field * span : (field + 1) * span] = low
        return carry

    lax.fori_loop(0, matrix_ref.shape[1] // (2 * rows), one, 0)


def span_kernel(counts_ref, coef_ref, u_ref, w_ref, out_ref, order, bands):
    rows, planes, width = u_ref.shape
    kept = out_ref.shape[0]

    @pl.when(pl.program_id(0) == 0)
    def _():
        list_fluid(counts_ref, order)
        band_rows(bands, coef_ref, order, HALF, planes)

    def some(index, carry):
        here = pl.ds(pl.multiple_of(index * HALF, HALF), HALF)
        u = u_ref[here].reshape(HALF * planes, width)
        w = w_ref[here].reshape(HALF * planes, width)
        flux = (u.astype(jnp.float32) * w.astype(jnp.float32)).astype(jnp.bfloat16)
        fields = jnp.concatenate([u, flux], axis=0)
        acc = jnp.dot(bands[0], fields, preferred_element_type=jnp.float32)
        acc = acc + jnp.dot(bands[1], fields, preferred_element_type=jnp.float32)
        out_ref[:, here] = acc.reshape(-1, HALF, width)[:kept]
        return carry

    lax.fori_loop(0, rows // HALF, some, 0)


def span_terms(counts, coef, u, w, kept):
    rows, planes, width = u.shape
    group = step_rows(rows)
    return pl.pallas_call(
        span_kernel,
        grid=(rows // group,),
        out_shape=jax.ShapeDtypeStruct((kept, rows, width), jnp.float32),
        in_specs=[
            pl.BlockSpec(memory_space=pltpu.SMEM),
            pl.BlockSpec(memory_space=pltpu.SMEM),
            pl.BlockSpec((group, planes, width), lambda i: (i, 0, 0)),
            pl.BlockSpec((group, planes, width), lambda i: (i, 0, 0)),
        ],
        out_specs=pl.BlockSpec((kept, group, width), lambda i: (0, i, 0)),
        scratch_shapes=[
            pltpu.SMEM((planes,), jnp.int32),
            pltpu.VMEM((2, even(kept) * HALF, 2 * HALF * planes), jnp.bfloat16),
        ],
        compiler_params=params(1),
        cost_estimate=NO_COST,
        name="span_terms",
    )(counts, coef, u, w)


def stream_kernel(spots_ref, *refs):
    *block_refs, first_ref, second_ref, span_ref, out_ref, matrix, both = refs
    group, rows, width = block_refs[0].shape
    own = first_ref.shape[0]
    places = len(block_refs)

    @pl.when(pl.program_id(0) == 0)
    def _():
        def prepare(place, carry):
            lane = pl.ds(pl.multiple_of(spots_ref[place] * width, width), width)

            def some(index, carry):
                row = pl.ds(pl.multiple_of(index * CHUNK, CHUNK), CHUNK)
                matrix[place, row, :width] = second_ref[row, lane] * jnp.bfloat16(VISCOSITY)
                matrix[place, row, width:] = -first_ref[row, lane]
                return carry

            return lax.fori_loop(0, own // CHUNK, some, carry)

        lax.fori_loop(0, places, prepare, 0)

    for place, ref in enumerate(block_refs):

        def square(slot, carry):
            u = ref[slot]
            full = u.astype(jnp.float32)
            row = pl.ds(pl.multiple_of(slot * rows, rows), rows)
            both[place, row, :width] = u
            both[place, row, width:] = (full * full).astype(jnp.bfloat16)
            return carry

        lax.fori_loop(0, group, square, 0)

    out_ref[...] = span_ref[...]

    def one(place, carry):
        part = lax.dot_general(
            both[place],
            matrix[place],
            (((1,), (1,)), ((), ())),
            preferred_element_type=jnp.float32,
        )
        out_ref[...] += part.reshape(out_ref.shape)
        return carry

    lax.fori_loop(0, places, one, 0)


def stream_terms(spots, blocks, first, second, span):
    kept, rows, width = blocks[0].shape
    own, total = first.shape
    group = min(4, kept)
    by_group = pl.BlockSpec((group, rows, width), lambda i: (i, 0, 0))
    whole = pl.BlockSpec((own, total), lambda i: (0, 0))
    return pl.pallas_call(
        stream_kernel,
        grid=(pl.cdiv(kept, group),),
        out_shape=jax.ShapeDtypeStruct((kept, rows, own), jnp.float32),
        in_specs=[pl.BlockSpec(memory_space=pltpu.SMEM)]
        + [by_group] * len(blocks)
        + [whole, whole, pl.BlockSpec((group, rows, own), lambda i: (i, 0, 0))],
        out_specs=pl.BlockSpec((group, rows, own), lambda i: (i, 0, 0)),
        scratch_shapes=[
            pltpu.VMEM((len(blocks), own, 2 * width), jnp.bfloat16),
            pltpu.VMEM((len(blocks), group * rows, 2 * width), jnp.bfloat16),
        ],
        compiler_params=params(1),
        cost_estimate=NO_COST,
        name="stream_terms",
    )(spots, *blocks, first, second, span)


def swap_rows(array, mask):
    count = lax.axis_size("row")
    return lax.ppermute(array, "row", [(row, row ^ mask) for row in range(count)])


def gather_rows(own, other):
    mask = lax.axis_size("row") // 2
    row = lax.axis_index("row")
    blocks, spots = [own, other], [row, row ^ mask]
    while mask > 1:
        mask //= 2
        blocks = blocks + [swap_rows(block, mask) for block in blocks]
        spots = spots + [spot ^ mask for spot in spots]
    return blocks, jnp.stack(spots).astype(jnp.int32)


def with_flux(pair):
    u, v = pair
    return u, (u.astype(jnp.float32) * v.astype(jnp.float32)).astype(jnp.bfloat16)


def abreast(group):
    return 2 if group % 2 == 0 else 1


def units_a_step(units):
    return next(g for g in (4, 6, 10, 2, 1) if units % g == 0)


def whole_kernel(matrix_ref, pair_ref, _, out_ref, lines):
    sources, group, _, rows, lanes = pair_ref.shape
    total = sources * rows
    side = abreast(group)

    def some(index, carry):
        for k in range(side):
            unit = index * side + k
            lane = slice(k * lanes, (k + 1) * lanes)
            u, flux = with_flux((pair_ref[:, unit, 0], pair_ref[:, unit, 1]))
            lines[:total, lane] = u.reshape(total, lanes)
            lines[total:, lane] = flux.reshape(total, lanes)
        terms = jnp.dot(matrix_ref[...], lines[...], preferred_element_type=jnp.float32)
        terms = terms.astype(jnp.bfloat16)
        for k in range(side):
            lane = slice(k * lanes, (k + 1) * lanes)
            out_ref[:, index * side + k] = terms[:, lane].reshape(sources, rows, lanes)
        return carry

    lax.fori_loop(0, group // side, some, 0)


def whole_terms(matrix, pairs, behind):
    sources, units, _, rows, lanes = pairs.shape
    group = units_a_step(units)
    return pl.pallas_call(
        whole_kernel,
        grid=(units // group,),
        out_shape=jax.ShapeDtypeStruct(behind.shape, behind.dtype),
        in_specs=[
            pl.BlockSpec(matrix.shape, lambda i: (0, 0)),
            pl.BlockSpec((sources, group, 2, rows, lanes), lambda i: (0, i, 0, 0, 0)),
            pl.BlockSpec(memory_space=pl.ANY),
        ],
        out_specs=pl.BlockSpec((sources, group, rows, lanes), lambda i: (0, i, 0, 0)),
        scratch_shapes=[pltpu.VMEM((2 * sources * rows, abreast(group) * lanes), jnp.bfloat16)],
        input_output_aliases={2: 0},
        compiler_params=params(1),
        cost_estimate=NO_COST,
        name="whole_terms",
    )(matrix, pairs, behind)


def half_kernel(spot_ref, matrix_ref, *refs):
    *pair_refs, out_ref, lines = refs
    group, _, rows, lanes = pair_refs[0].shape
    side = abreast(group)
    half = len(pair_refs) * rows
    on_u = pl.ds(pl.multiple_of(spot_ref[1] * half, half), half)
    on_flux = pl.ds(pl.multiple_of((2 + spot_ref[1]) * half, half), half)

    def some(index, carry):
        for mask, ref in enumerate(pair_refs):
            start = pl.multiple_of((spot_ref[0] ^ mask) * rows, rows)
            for k in range(side):
                unit = index * side + k
                lane = slice(k * lanes, (k + 1) * lanes)
                u, flux = with_flux((ref[unit, 0], ref[unit, 1]))
                lines[pl.ds(start, rows), lane] = u
                lines[pl.ds(pl.multiple_of(half + start, rows), rows), lane] = flux
        terms = jnp.dot(matrix_ref[:, on_u], lines[:half], preferred_element_type=jnp.float32)
        terms = terms + jnp.dot(
            matrix_ref[:, on_flux], lines[half:], preferred_element_type=jnp.float32
        )
        terms = terms.astype(jnp.bfloat16)
        for k in range(side):
            lane = slice(k * lanes, (k + 1) * lanes)
            out_ref[:, index * side + k] = terms[:, lane].reshape(-1, rows, lanes)
        return carry

    lax.fori_loop(0, group // side, some, 0)


def half_terms(spot, matrix, pairs, before):
    near = len(pairs)
    units, _, rows, lanes = pairs[0].shape
    group = units_a_step(before)
    side = abreast(group)
    return pl.pallas_call(
        half_kernel,
        grid=(pl.cdiv(units, group),),
        out_shape=jax.ShapeDtypeStruct((2 * near, before + units, rows, lanes), jnp.bfloat16),
        in_specs=[
            pl.BlockSpec(memory_space=pltpu.SMEM),
            pl.BlockSpec(matrix.shape, lambda i: (0, 0)),
        ]
        + [pl.BlockSpec((group, 2, rows, lanes), lambda i: (i, 0, 0, 0))] * near,
        out_specs=pl.BlockSpec(
            (2 * near, group, rows, lanes), lambda i: (0, before // group + i, 0, 0)
        ),
        scratch_shapes=[pltpu.VMEM((2 * near * rows, side * lanes), jnp.bfloat16)],
        compiler_params=params(1),
        cost_estimate=HIGH_COST,
        name="half_terms",
    )(spot, matrix, *pairs)


def finish_kernel(apart, counts_ref, base_ref, wall_ref, out_ref, order, chosen, placed):
    rows, planes, width = out_ref.shape
    kept = base_ref.shape[0]
    places, units, _, lanes = wall_ref.shape
    parts = width // lanes
    whole = parts * apart // places

    @pl.when(pl.program_id(0) == 0)
    def _():
        found = list_fluid(counts_ref, order)
        one_hot_rows(chosen, order, HALF, planes, found)
        placed[...] = chosen[...].T

    def some(index, carry):
        here = pl.ds(pl.multiple_of(index * ROWS, ROWS), ROWS)
        columns = []
        for part in range(parts):
            first = part * places // parts
            pieces = [wall_ref[first + k, :whole, here] for k in range(places // parts)]
            column = jnp.concatenate(pieces, axis=0).astype(jnp.float32)
            if units > whole:
                low = wall_ref[part, whole:, here].astype(jnp.float32)
                high = wall_ref[part + parts, whole:, here].astype(jnp.float32)
                column = jnp.concatenate([column, low + high], axis=0)
            columns.append(column)
        value = base_ref[:, here] + jnp.concatenate(columns, axis=-1)
        if kept % 2 == 1:
            value = jnp.concatenate([value, jnp.zeros((1, ROWS, width), jnp.float32)], axis=0)
        for start in range(0, ROWS, HALF):
            some_rows = value[:, start : start + HALF].reshape(-1, width)
            out = jnp.dot(
                placed[...], some_rows.astype(jnp.bfloat16), preferred_element_type=jnp.float32
            )
            out_ref[pl.ds(index * ROWS + start, HALF)] = out.astype(jnp.bfloat16).reshape(
                HALF, planes, width
            )
        return carry

    lax.fori_loop(0, rows // ROWS, some, 0)


def finish(counts, base, wall, planes, apart):
    kept, rows, width = base.shape
    places, units, _, lanes = wall.shape
    group = step_rows(rows)
    return pl.pallas_call(
        functools.partial(finish_kernel, apart),
        grid=(rows // group,),
        out_shape=jax.ShapeDtypeStruct((rows, planes, width), jnp.bfloat16),
        in_specs=[
            pl.BlockSpec(memory_space=pltpu.SMEM),
            pl.BlockSpec((kept, group, width), lambda i: (0, i, 0)),
            pl.BlockSpec((places, units, group, lanes), lambda i: (0, 0, i, 0)),
        ],
        out_specs=pl.BlockSpec((group, planes, width), lambda i: (i, 0, 0)),
        scratch_shapes=[
            pltpu.SMEM((planes,), jnp.int32),
            pltpu.VMEM((even(kept) * HALF, HALF * planes), jnp.bfloat16),
            pltpu.VMEM((HALF * planes, even(kept) * HALF), jnp.bfloat16),
        ],
        compiler_params=params(1),
        cost_estimate=NO_COST,
        name="finish",
    )(counts, base, wall)


def swap(array, mask):
    count = lax.axis_size("col")
    if mask == 0:
        return array
    return lax.ppermute(array, "col", [(column, column ^ mask) for column in range(count)])


def with_kept(
    apart, kept, spot, u, v, w, first, second, wall_first, wall_second, metric1, metric2, coef, counts
):
    rows, planes, width = u.shape
    columns = lax.axis_size("col")
    near = columns // 2
    own, pairs, *halves = pack(counts, spot, u, v, apart, kept, near)
    parts, _, _, _, lanes = pairs.shape
    units = parts * apart // columns
    halves = [swap(half, mask) for mask, half in enumerate(halves)]
    if halves:
        pairs, halves[1] = lax.optimization_barrier((pairs, halves[1]))
    lines = lax.all_to_all(
        pairs.reshape(columns, units, 2, rows, lanes), "col", split_axis=0, concat_axis=0
    )
    one, two = metric1[:, None], metric2[:, None]
    wide_first = wall_first.astype(jnp.float32)
    on_stream = VISCOSITY * (one * one * wall_second.astype(jnp.float32) + two * wide_first)
    matrix = jnp.concatenate([on_stream, -one * wide_first], axis=1).astype(jnp.bfloat16)
    first_block = swap_rows(own, lax.axis_size("row") // 2)
    if halves:
        wall = half_terms(spot, matrix, halves, units)
    else:
        wall = jnp.zeros((columns, units, rows, lanes), jnp.bfloat16)
    lines, wall, first_block = lax.optimization_barrier((lines, wall, first_block))
    wall = whole_terms(matrix, lines, wall)
    wall = lax.all_to_all(wall, "col", split_axis=0, concat_axis=0)
    blocks, spots = gather_rows(own, first_block)
    span = span_terms(counts, coef, u, w, kept)
    base = stream_terms(spots, blocks, first, second, span)
    return finish(counts, base, wall, planes, apart)


def share_of(kept, parts, columns):
    if 2 * parts != columns:
        return kept
    options = range(columns // 2, kept + 1, columns // 2)
    return min(options, key=lambda a: max(12 + 2 * a, 2 + kept + a / 2) - 1.01 * a)


def on_device(u, v, w, first, second, wall_first, wall_second, metric1, metric2, coef, counts):
    u, v, w = (jnp.swapaxes(t, 1, 2) for t in (u, v, w))
    planes, width = u.shape[1:]
    columns = lax.axis_size("col")
    parts = width // unit_lanes(width)
    step = 1 if 2 * parts == columns else columns // math.gcd(columns, parts)
    blocks = counts.shape[0]
    least, middle = blocks - 1 + ZB, (blocks - 1) * (ZB + 1) / 2 + ZB
    sizes = [size for size in range(step, planes, step) if size >= least]
    sizes = [size for size in sizes if -4 < (size - middle) / step < 5] + [planes]
    branches = [
        functools.partial(with_kept, share_of(size, parts, columns), size) for size in sizes
    ]
    fluid = jnp.sum(counts)
    index = (fluid - sizes[0] + (step - 1)) // step
    column, near = lax.axis_index("col"), columns // 2
    spot = jnp.stack([column % near, column // near]).astype(jnp.int32)
    operands = (spot, u, v, w, first, second, wall_first, wall_second, metric1, metric2, coef, counts)
    out = lax.switch(index, branches, *operands)
    return jnp.swapaxes(out, 1, 2)


def solution(mesh):
    field = P("col", "row", None)
    placed = (field, field, field, P("row", None), P("row", None)) + (P(),) * 6
    return jax.shard_map(
        on_device,
        mesh=mesh,
        in_specs=placed,
        out_specs=field,
        check_vma=False,
    )
```

```python
import functools
import math

import jax
import jax.numpy as jnp
from jax import lax
from jax.experimental import pallas as pl
from jax.experimental.pallas import tpu as pltpu
from jax.sharding import PartitionSpec as P

ZB = 4
LANES = 128
ROWS = 16
HALF = 8
CHUNK = 32
VISCOSITY = 0.25
VMEM_BYTES = 65280 * 1024
NO_COST = pl.CostEstimate(flops=0, bytes_accessed=0, transcendentals=0)
HIGH_COST = pl.CostEstimate(flops=10**12, bytes_accessed=10**9, transcendentals=0)


def params(steps):
    return pltpu.CompilerParams(
        dimension_semantics=("arbitrary",) * steps, vmem_limit_bytes=VMEM_BYTES
    )


def unit_lanes(width):
    return LANES if width % LANES == 0 else width


def even(kept):
    return kept + kept % 2


def step_rows(rows):
    return next(g for g in (2 * ROWS, ROWS, rows) if rows % g == 0)


def list_fluid(counts_ref, order_ref):
    planes = order_ref.shape[0]

    def clear(plane, carry):
        order_ref[plane] = 0
        return carry

    lax.fori_loop(0, planes, clear, 0)

    def visit(plane, filled):
        fluid = lax.rem(plane, ZB) < counts_ref[plane // ZB]

        @pl.when(fluid)
        def _():
            order_ref[filled] = plane

        return filled + fluid.astype(jnp.int32)

    return lax.fori_loop(0, planes, visit, 0)


def one_hot_rows(matrix_ref, order, rows, planes, found):
    spread = (2 * rows, rows * planes)
    row = lax.broadcasted_iota(jnp.int32, spread, 0)
    later = row >= rows
    near = lax.broadcasted_iota(jnp.int32, spread, 1) - planes * jnp.where(later, row - rows, row)

    def one(pair, carry):
        slot = 2 * pair
        here = jnp.where(slot < found, order[slot], -rows * planes)
        after = jnp.where(slot + 1 < found, order[slot + 1], -rows * planes)
        hot = jnp.where(near == jnp.where(later, after, here), 1.0, 0.0).astype(jnp.bfloat16)
        start = pl.multiple_of(slot * rows, 2 * rows)
        matrix_ref[pl.ds(start, 2 * rows), :] = hot
        return carry

    lax.fori_loop(0, matrix_ref.shape[0] // (2 * rows), one, 0)


def pack_kernel(counts_ref, spot_ref, u_ref, v_ref, own_ref, pair_ref, *refs):
    *half_refs, order, chosen, rest = refs
    rows, planes, width = u_ref.shape
    kept = own_ref.shape[0]
    parts, apart, _, _, lanes = pair_ref.shape

    @pl.when(pl.program_id(0) == 0)
    def _():
        found = list_fluid(counts_ref, order)
        one_hot_rows(chosen, order, HALF, planes, found)

    def select(ref, first):
        picked = []
        for start in range(0, ROWS, HALF):
            flat = ref[pl.ds(first + start, HALF)].reshape(HALF * planes, width)
            part = jnp.dot(chosen[...], flat, preferred_element_type=jnp.float32)
            picked.append(part.reshape(-1, HALF, width)[:kept])
        return jnp.concatenate(picked, axis=1).astype(jnp.bfloat16)

    def some(index, carry):
        first = pl.multiple_of(index * ROWS, ROWS)
        here = pl.ds(first, ROWS)
        for field, ref in enumerate((u_ref, v_ref)):
            value = select(ref, first)
            if field == 0:
                own_ref[:, here] = value
            for part in range(parts):
                lane = slice(part * lanes, (part + 1) * lanes)
                pair_ref[part, :, field, here] = value[:apart, :, lane]
            if half_refs:
                rest[...] = value[apart:]
            for mask, half_ref in enumerate(half_refs):
                start = pl.multiple_of((spot_ref[0] ^ mask) * lanes, lanes)
                half_ref[:, field, here] = rest[:, :, pl.ds(start, lanes)]
        return carry

    lax.fori_loop(0, rows // ROWS, some, 0)


def pack(counts, spot, u, v, apart, kept, near):
    rows, planes, width = u.shape
    lanes = unit_lanes(width)
    parts = width // lanes
    group = step_rows(rows)
    others = kept - apart
    halves = near if others > 0 else 0
    return pl.pallas_call(
        pack_kernel,
        grid=(rows // group,),
        out_shape=[
            jax.ShapeDtypeStruct((kept, rows, width), jnp.bfloat16),
            jax.ShapeDtypeStruct((parts, apart, 2, rows, lanes), jnp.bfloat16),
        ]
        + [jax.ShapeDtypeStruct((others, 2, rows, lanes), jnp.bfloat16)] * halves,
        in_specs=[
            pl.BlockSpec(memory_space=pltpu.SMEM),
            pl.BlockSpec(memory_space=pltpu.SMEM),
            pl.BlockSpec((group, planes, width), lambda i: (i, 0, 0)),
            pl.BlockSpec((group, planes, width), lambda i: (i, 0, 0)),
        ],
        out_specs=[
            pl.BlockSpec((kept, group, width), lambda i: (0, i, 0)),
            pl.BlockSpec((parts, apart, 2, group, lanes), lambda i: (0, 0, 0, i, 0)),
        ]
        + [pl.BlockSpec((others, 2, group, lanes), lambda i: (0, 0, i, 0))] * halves,
        scratch_shapes=[
            pltpu.SMEM((planes,), jnp.int32),
            pltpu.VMEM((even(kept) * HALF, HALF * planes), jnp.bfloat16),
            pltpu.VMEM((max(others, 1), ROWS, width), jnp.bfloat16),
        ],
        compiler_params=params(1),
        cost_estimate=NO_COST,
        name="pack",
    )(counts, spot, u, v)


def band_rows(matrix_ref, coef_ref, order, rows, planes):
    taps = coef_ref.shape[1]
    span = rows * planes
    spread = (2 * rows, span)
    row = lax.broadcasted_iota(jnp.int32, spread, 0)
    later = row >= rows
    plane = lax.broadcasted_iota(jnp.int32, spread, 1) - planes * jnp.where(later, row - rows, row)
    inside = (plane >= 0) & (plane < planes)

    def one(pair, carry):
        slot = 2 * pair
        ahead = plane - jnp.where(later, order[slot + 1], order[slot]) + taps // 2
        ahead = jnp.where(ahead < 0, ahead + planes, ahead)
        ahead = jnp.where(ahead >= planes, ahead - planes, ahead)
        ahead = jnp.where(inside, ahead, -1)
        start = pl.multiple_of(slot * rows, 2 * rows)

        def tap(index, values):
            hit = ahead == index
            on_u, on_f = VISCOSITY * coef_ref[1, index], -coef_ref[0, index]
            return (
                values[0] + jnp.where(hit, on_u, 0.0),
                values[1] + jnp.where(hit, on_f, 0.0),
            )

        zero = jnp.zeros(spread, jnp.float32)
        for field, value in enumerate(lax.fori_loop(0, taps, tap, (zero, zero), unroll=True)):
            high = value.astype(jnp.bfloat16)
            low = (value - high.astype(jnp.float32)).astype(jnp.bfloat16)
            matrix_ref[0, pl.ds(start, 2 * rows), field * span : (field + 1) * span] = high
            matrix_ref[1, pl.ds(start, 2 * rows), field * span : (field + 1) * span] = low
        return carry

    lax.fori_loop(0, matrix_ref.shape[1] // (2 * rows), one, 0)


def span_kernel(counts_ref, coef_ref, u_ref, w_ref, out_ref, order, bands):
    rows, planes, width = u_ref.shape
    kept = out_ref.shape[0]

    @pl.when(pl.program_id(0) == 0)
    def _():
        list_fluid(counts_ref, order)
        band_rows(bands, coef_ref, order, HALF, planes)

    def some(index, carry):
        here = pl.ds(pl.multiple_of(index * HALF, HALF), HALF)
        u = u_ref[here].reshape(HALF * planes, width)
        w = w_ref[here].reshape(HALF * planes, width)
        flux = (u.astype(jnp.float32) * w.astype(jnp.float32)).astype(jnp.bfloat16)
        fields = jnp.concatenate([u, flux], axis=0)
        acc = jnp.dot(bands[0], fields, preferred_element_type=jnp.float32)
        acc = acc + jnp.dot(bands[1], fields, preferred_element_type=jnp.float32)
        out_ref[:, here] = acc.reshape(-1, HALF, width)[:kept]
        return carry

    lax.fori_loop(0, rows // HALF, some, 0)


def span_terms(counts, coef, u, w, kept):
    rows, planes, width = u.shape
    group = step_rows(rows)
    return pl.pallas_call(
        span_kernel,
        grid=(rows // group,),
        out_shape=jax.ShapeDtypeStruct((kept, rows, width), jnp.float32),
        in_specs=[
            pl.BlockSpec(memory_space=pltpu.SMEM),
            pl.BlockSpec(memory_space=pltpu.SMEM),
            pl.BlockSpec((group, planes, width), lambda i: (i, 0, 0)),
            pl.BlockSpec((group, planes, width), lambda i: (i, 0, 0)),
        ],
        out_specs=pl.BlockSpec((kept, group, width), lambda i: (0, i, 0)),
        scratch_shapes=[
            pltpu.SMEM((planes,), jnp.int32),
            pltpu.VMEM((2, even(kept) * HALF, 2 * HALF * planes), jnp.bfloat16),
        ],
        compiler_params=params(1),
        cost_estimate=NO_COST,
        name="span_terms",
    )(counts, coef, u, w)


def stream_kernel(spots_ref, *refs):
    *block_refs, first_ref, second_ref, span_ref, out_ref, matrix, both = refs
    group, rows, width = block_refs[0].shape
    own = first_ref.shape[0]
    places = len(block_refs)

    @pl.when(pl.program_id(0) == 0)
    def _():
        def prepare(place, carry):
            lane = pl.ds(pl.multiple_of(spots_ref[place] * width, width), width)

            def some(index, carry):
                row = pl.ds(pl.multiple_of(index * CHUNK, CHUNK), CHUNK)
                matrix[place, row, :width] = second_ref[row, lane] * jnp.bfloat16(VISCOSITY)
                matrix[place, row, width:] = -first_ref[row, lane]
                return carry

            return lax.fori_loop(0, own // CHUNK, some, carry)

        lax.fori_loop(0, places, prepare, 0)

    for place, ref in enumerate(block_refs):

        def square(slot, carry):
            u = ref[slot]
            full = u.astype(jnp.float32)
            row = pl.ds(pl.multiple_of(slot * rows, rows), rows)
            both[place, row, :width] = u
            both[place, row, width:] = (full * full).astype(jnp.bfloat16)
            return carry

        lax.fori_loop(0, group, square, 0)

    out_ref[...] = span_ref[...]

    def one(place, carry):
        part = lax.dot_general(
            both[place],
            matrix[place],
            (((1,), (1,)), ((), ())),
            preferred_element_type=jnp.float32,
        )
        out_ref[...] += part.reshape(out_ref.shape)
        return carry

    lax.fori_loop(0, places, one, 0)


def stream_terms(spots, blocks, first, second, span):
    kept, rows, width = blocks[0].shape
    own, total = first.shape
    group = min(4, kept)
    by_group = pl.BlockSpec((group, rows, width), lambda i: (i, 0, 0))
    whole = pl.BlockSpec((own, total), lambda i: (0, 0))
    return pl.pallas_call(
        stream_kernel,
        grid=(pl.cdiv(kept, group),),
        out_shape=jax.ShapeDtypeStruct((kept, rows, own), jnp.float32),
        in_specs=[pl.BlockSpec(memory_space=pltpu.SMEM)]
        + [by_group] * len(blocks)
        + [whole, whole, pl.BlockSpec((group, rows, own), lambda i: (i, 0, 0))],
        out_specs=pl.BlockSpec((group, rows, own), lambda i: (i, 0, 0)),
        scratch_shapes=[
            pltpu.VMEM((len(blocks), own, 2 * width), jnp.bfloat16),
            pltpu.VMEM((len(blocks), group * rows, 2 * width), jnp.bfloat16),
        ],
        compiler_params=params(1),
        cost_estimate=NO_COST,
        name="stream_terms",
    )(spots, *blocks, first, second, span)


def swap_rows(array, mask):
    count = lax.axis_size("row")
    return lax.ppermute(array, "row", [(row, row ^ mask) for row in range(count)])


def gather_rows(own, other):
    mask = lax.axis_size("row") // 2
    row = lax.axis_index("row")
    blocks, spots = [own, other], [row, row ^ mask]
    while mask > 1:
        mask //= 2
        blocks = blocks + [swap_rows(block, mask) for block in blocks]
        spots = spots + [spot ^ mask for spot in spots]
    return blocks, jnp.stack(spots).astype(jnp.int32)


def with_flux(pair):
    u, v = pair
    return u, (u.astype(jnp.float32) * v.astype(jnp.float32)).astype(jnp.bfloat16)


def abreast(group):
    return 2 if group % 2 == 0 else 1


def units_a_step(units):
    return next(g for g in (4, 6, 10, 2, 1) if units % g == 0)


def whole_kernel(matrix_ref, pair_ref, _, out_ref, lines):
    sources, group, _, rows, lanes = pair_ref.shape
    total = sources * rows
    side = abreast(group)

    def some(index, carry):
        for k in range(side):
            unit = index * side + k
            lane = slice(k * lanes, (k + 1) * lanes)
            u, flux = with_flux((pair_ref[:, unit, 0], pair_ref[:, unit, 1]))
            lines[:total, lane] = u.reshape(total, lanes)
            lines[total:, lane] = flux.reshape(total, lanes)
        terms = jnp.dot(matrix_ref[...], lines[...], preferred_element_type=jnp.float32)
        terms = terms.astype(jnp.bfloat16)
        for k in range(side):
            lane = slice(k * lanes, (k + 1) * lanes)
            out_ref[:, index * side + k] = terms[:, lane].reshape(sources, rows, lanes)
        return carry

    lax.fori_loop(0, group // side, some, 0)


def whole_terms(matrix, pairs, behind):
    sources, units, _, rows, lanes = pairs.shape
    group = units_a_step(units)
    return pl.pallas_call(
        whole_kernel,
        grid=(units // group,),
        out_shape=jax.ShapeDtypeStruct(behind.shape, behind.dtype),
        in_specs=[
            pl.BlockSpec(matrix.shape, lambda i: (0, 0)),
            pl.BlockSpec((sources, group, 2, rows, lanes), lambda i: (0, i, 0, 0, 0)),
            pl.BlockSpec(memory_space=pl.ANY),
        ],
        out_specs=pl.BlockSpec((sources, group, rows, lanes), lambda i: (0, i, 0, 0)),
        scratch_shapes=[pltpu.VMEM((2 * sources * rows, abreast(group) * lanes), jnp.bfloat16)],
        input_output_aliases={2: 0},
        compiler_params=params(1),
        cost_estimate=NO_COST,
        name="whole_terms",
    )(matrix, pairs, behind)


def half_kernel(spot_ref, matrix_ref, *refs):
    *pair_refs, out_ref, lines = refs
    group, _, rows, lanes = pair_refs[0].shape
    side = abreast(group)
    half = len(pair_refs) * rows
    on_u = pl.ds(pl.multiple_of(spot_ref[1] * half, half), half)
    on_flux = pl.ds(pl.multiple_of((2 + spot_ref[1]) * half, half), half)

    def some(index, carry):
        for mask, ref in enumerate(pair_refs):
            start = pl.multiple_of((spot_ref[0] ^ mask) * rows, rows)
            for k in range(side):
                unit = index * side + k
                lane = slice(k * lanes, (k + 1) * lanes)
                u, flux = with_flux((ref[unit, 0], ref[unit, 1]))
                lines[pl.ds(start, rows), lane] = u
                lines[pl.ds(pl.multiple_of(half + start, rows), rows), lane] = flux
        terms = jnp.dot(matrix_ref[:, on_u], lines[:half], preferred_element_type=jnp.float32)
        terms = terms + jnp.dot(
            matrix_ref[:, on_flux], lines[half:], preferred_element_type=jnp.float32
        )
        terms = terms.astype(jnp.bfloat16)
        for k in range(side):
            lane = slice(k * lanes, (k + 1) * lanes)
            out_ref[:, index * side + k] = terms[:, lane].reshape(-1, rows, lanes)
        return carry

    lax.fori_loop(0, group // side, some, 0)


def half_terms(spot, matrix, pairs, before):
    near = len(pairs)
    units, _, rows, lanes = pairs[0].shape
    group = units_a_step(before)
    side = abreast(group)
    return pl.pallas_call(
        half_kernel,
        grid=(pl.cdiv(units, group),),
        out_shape=jax.ShapeDtypeStruct((2 * near, before + units, rows, lanes), jnp.bfloat16),
        in_specs=[
            pl.BlockSpec(memory_space=pltpu.SMEM),
            pl.BlockSpec(matrix.shape, lambda i: (0, 0)),
        ]
        + [pl.BlockSpec((group, 2, rows, lanes), lambda i: (i, 0, 0, 0))] * near,
        out_specs=pl.BlockSpec(
            (2 * near, group, rows, lanes), lambda i: (0, before // group + i, 0, 0)
        ),
        scratch_shapes=[pltpu.VMEM((2 * near * rows, side * lanes), jnp.bfloat16)],
        compiler_params=params(1),
        cost_estimate=HIGH_COST,
        name="half_terms",
    )(spot, matrix, *pairs)


def finish_kernel(apart, counts_ref, base_ref, wall_ref, out_ref, order, chosen, placed):
    rows, planes, width = out_ref.shape
    kept = base_ref.shape[0]
    places, units, _, lanes = wall_ref.shape
    parts = width // lanes
    whole = parts * apart // places

    @pl.when(pl.program_id(0) == 0)
    def _():
        found = list_fluid(counts_ref, order)
        one_hot_rows(chosen, order, HALF, planes, found)
        placed[...] = chosen[...].T

    def some(index, carry):
        here = pl.ds(pl.multiple_of(index * ROWS, ROWS), ROWS)
        columns = []
        for part in range(parts):
            first = part * places // parts
            pieces = [wall_ref[first + k, :whole, here] for k in range(places // parts)]
            column = jnp.concatenate(pieces, axis=0).astype(jnp.float32)
            if units > whole:
                low = wall_ref[part, whole:, here].astype(jnp.float32)
                high = wall_ref[part + parts, whole:, here].astype(jnp.float32)
                column = jnp.concatenate([column, low + high], axis=0)
            columns.append(column)
        value = base_ref[:, here] + jnp.concatenate(columns, axis=-1)
        if kept % 2 == 1:
            value = jnp.concatenate([value, jnp.zeros((1, ROWS, width), jnp.float32)], axis=0)
        for start in range(0, ROWS, HALF):
            some_rows = value[:, start : start + HALF].reshape(-1, width)
            out = jnp.dot(
                placed[...], some_rows.astype(jnp.bfloat16), preferred_element_type=jnp.float32
            )
            out_ref[pl.ds(index * ROWS + start, HALF)] = out.astype(jnp.bfloat16).reshape(
                HALF, planes, width
            )
        return carry

    lax.fori_loop(0, rows // ROWS, some, 0)


def finish(counts, base, wall, planes, apart):
    kept, rows, width = base.shape
    places, units, _, lanes = wall.shape
    group = step_rows(rows)
    return pl.pallas_call(
        functools.partial(finish_kernel, apart),
        grid=(rows // group,),
        out_shape=jax.ShapeDtypeStruct((rows, planes, width), jnp.bfloat16),
        in_specs=[
            pl.BlockSpec(memory_space=pltpu.SMEM),
            pl.BlockSpec((kept, group, width), lambda i: (0, i, 0)),
            pl.BlockSpec((places, units, group, lanes), lambda i: (0, 0, i, 0)),
        ],
        out_specs=pl.BlockSpec((group, planes, width), lambda i: (i, 0, 0)),
        scratch_shapes=[
            pltpu.SMEM((planes,), jnp.int32),
            pltpu.VMEM((even(kept) * HALF, HALF * planes), jnp.bfloat16),
            pltpu.VMEM((HALF * planes, even(kept) * HALF), jnp.bfloat16),
        ],
        compiler_params=params(1),
        cost_estimate=NO_COST,
        name="finish",
    )(counts, base, wall)


def swap(array, mask):
    count = lax.axis_size("col")
    if mask == 0:
        return array
    return lax.ppermute(array, "col", [(column, column ^ mask) for column in range(count)])


def with_kept(
    apart, kept, spot, u, v, w, first, second, wall_first, wall_second, metric1, metric2, coef, counts
):
    rows, planes, width = u.shape
    columns = lax.axis_size("col")
    near = columns // 2
    own, pairs, *halves = pack(counts, spot, u, v, apart, kept, near)
    parts, _, _, _, lanes = pairs.shape
    units = parts * apart // columns
    halves = [swap(half, mask) for mask, half in enumerate(halves)]
    if halves:
        pairs, halves[1] = lax.optimization_barrier((pairs, halves[1]))
    lines = lax.all_to_all(
        pairs.reshape(columns, units, 2, rows, lanes), "col", split_axis=0, concat_axis=0
    )
    one, two = metric1[:, None], metric2[:, None]
    wide_first = wall_first.astype(jnp.float32)
    on_stream = VISCOSITY * (one * one * wall_second.astype(jnp.float32) + two * wide_first)
    matrix = jnp.concatenate([on_stream, -one * wide_first], axis=1).astype(jnp.bfloat16)
    first_block = swap_rows(own, lax.axis_size("row") // 2)
    if halves:
        wall = half_terms(spot, matrix, halves, units)
    else:
        wall = jnp.zeros((columns, units, rows, lanes), jnp.bfloat16)
    lines, wall, first_block = lax.optimization_barrier((lines, wall, first_block))
    wall = whole_terms(matrix, lines, wall)
    wall = lax.all_to_all(wall, "col", split_axis=0, concat_axis=0)
    blocks, spots = gather_rows(own, first_block)
    span = span_terms(counts, coef, u, w, kept)
    base = stream_terms(spots, blocks, first, second, span)
    return finish(counts, base, wall, planes, apart)


def share_of(kept, parts, columns):
    if 2 * parts != columns:
        return kept
    options = range(columns // 2, kept + 1, columns // 2)
    return min(options, key=lambda a: max(12 + 2 * a, 2 + kept + a / 2) - 1.01 * a)


def on_device(u, v, w, first, second, wall_first, wall_second, metric1, metric2, coef, counts):
    u, v, w = (jnp.swapaxes(t, 1, 2) for t in (u, v, w))
    planes, width = u.shape[1:]
    columns = lax.axis_size("col")
    parts = width // unit_lanes(width)
    step = 1 if 2 * parts == columns else columns // math.gcd(columns, parts)
    blocks = counts.shape[0]
    least, middle = blocks - 1 + ZB, (blocks - 1) * (ZB + 1) / 2 + ZB
    sizes = [size for size in range(step, planes, step) if size >= least]
    sizes = [size for size in sizes if -4 < (size - middle) / step < 5] + [planes]
    branches = [
        functools.partial(with_kept, share_of(size, parts, columns), size) for size in sizes
    ]
    fluid = jnp.sum(counts)
    index = (fluid - sizes[0] + (step - 1)) // step
    column, near = lax.axis_index("col"), columns // 2
    spot = jnp.stack([column % near, column // near]).astype(jnp.int32)
    operands = (spot, u, v, w, first, second, wall_first, wall_second, metric1, metric2, coef, counts)
    out = lax.switch(index, branches, *operands)
    return jnp.swapaxes(out, 1, 2)


def solution(mesh):
    field = P("col", "row", None)
    placed = (field, field, field, P("row", None), P("row", None)) + (P(),) * 6
    return jax.shard_map(
        on_device,
        mesh=mesh,
        in_specs=placed,
        out_specs=field,
        check_vma=False,
    )
```
